32 devices in a mesh: gx: 8 (over z, x), gy: 2 (over core), gz: 2 (over y).
Axes of the slice: x: 2, y: 2, z: 4, core: 2. Of those that a mesh axis runs over, the one named last changes fastest.
Arguments:
- e_start: float32 [3, 64, 32, 256], P(None, 'gx', 'gy', 'gz'), may hold values from -6 to 6
- h_start: float32 [3, 64, 32, 256], P(None, 'gx', 'gy', 'gz'), may hold values from -6 to 6
- inv_perm: float32 [3, 64, 32, 256], P(None, 'gx', 'gy', 'gz'), may hold values from 0.25 to 1
- adj_seed: float32 [3, 64, 32, 256], P(None, 'gx', 'gy', 'gz'), may hold values from -6 to 6
- region_ids: int32 [64, 32, 256], P('gx', 'gy', 'gz'), may hold values from 0 to 255, as said below
Outputs:
- e_final: float32 [3, 64, 32, 256], P(None, 'gx', 'gy', 'gz')
- region_grad: float32 [3, 256], P(None, ('gx', 'gy', 'gz'))
The draws below stay inside these ranges and needn't reach their ends.
Inputs may be any that keep to these rules, and one draw needn't show every extreme that they name: `region_ids`: devices are numbered with gx slowest and gz fastest; region r is owned by device r // 8. Each region's cells lie within the tiles of two neighbouring devices along gx that share their gy and gz indices, the first with an even gx index, and the region is owned by one of those two devices.
All inputs are finite; a program needn't handle non-finite values.
Results may differ from the reference program's by a relative error of at most 0.00013.
Values sent between devices are 32-bit elements; how exact they have to be, the bound alone decides.
No kernel may reach another device: no remote copies, remote signals or barrier semaphores. Data moves between devices by JAX's collectives and lax.ppermute only.
A program may use at most 64 MiB of HBM per device.

```python
import math
import jax
import jax.numpy as jnp
from jax import lax

CX = 8
CY = 16
CZ = 128
STEPS = 4
REG_DEV = 8
NX = 64
NY = 32
NZ = 256
REGIONS = 256
N_GY = 2
N_GZ = 2


def draw_region_ids(key, part):
    shape_all = (NX, NY, NZ)
    x_cells = lax.broadcasted_iota(jnp.int32, shape_all, 0)
    y_cells = lax.broadcasted_iota(jnp.int32, shape_all, 1)
    z_cells = lax.broadcasted_iota(jnp.int32, shape_all, 2)
    first_owner = x_cells // (2 * CX) * (2 * N_GY * N_GZ) + y_cells // CY * N_GZ + z_cells // CZ
    second_owner = first_owner + N_GY * N_GZ
    first_key = jax.random.fold_in(key, 11)
    second_key = jax.random.fold_in(key, 23)
    first_pick = jax.random.randint(first_key, shape_all, 0, 2 * REG_DEV)
    second_pick = jax.random.randint(second_key, shape_all, 0, 2 * REG_DEV)
    local_ids = jnp.minimum(first_pick, second_pick)
    region = jnp.where(local_ids < REG_DEV, first_owner * REG_DEV + local_ids, second_owner * REG_DEV + local_ids - REG_DEV)
    last_cell = (x_cells == NX - 1) & (y_cells == NY - 1) & (z_cells == NZ - 1)
    first_cell = (x_cells == 0) & (y_cells == 0) & (z_cells == 0)
    region = jnp.where(last_cell, REGIONS - 1, region)
    region = jnp.where(first_cell, 0, region)
    return region.astype(jnp.int32)


def levels(own_key, dims, shards, least, top_value):
    loudness = 1.0
    for position, parts in shards:
        draws = jax.random.uniform(jax.random.fold_in(jax.random.fold_in(own_key, 6), position), (parts,), jnp.float32, least / len(shards), top_value / len(shards))
        loudness = loudness * jnp.repeat(jnp.exp(draws), dims[position] // parts).reshape((-1,) + (1,) * (len(dims) - 1 - position))
    return loudness


def normal_values(stream_key, dims, width, reach, split=(), dtype=jnp.bfloat16):
    level = levels(stream_key, dims, split, -0.22, 0.18) if split else 1.0
    result = jax.random.normal(stream_key, dims, jnp.float32) * width * level
    return jnp.minimum(jnp.maximum(result, -reach), reach).astype(dtype)


def setup_inputs(seed: int = 0) -> dict:
    arg_keys = jax.random.split(jax.random.key(seed), 6)
    e_start = normal_values(arg_keys[0], (3, NX, NY, NZ), 1.0, 6.0, ((1, 8), (2, 2), (3, 2)), jnp.float32)
    h_start = normal_values(arg_keys[1], (3, NX, NY, NZ), 1.0, 6.0, ((1, 8), (2, 2), (3, 2)), jnp.float32)
    inv_perm = jnp.clip(jnp.exp(math.log(1.0) - 1.3862944 * jax.random.uniform(arg_keys[2], (3, NX, NY, NZ), jnp.float32) ** levels(arg_keys[2], (3, NX, NY, NZ), ((1, 8), (2, 2), (3, 2)), -0.2, 0.2)), 0.25, 1.0)
    adj_seed = normal_values(arg_keys[3], (3, NX, NY, NZ), 1.0, 6.0, ((1, 8), (2, 2), (3, 2)), jnp.float32)
    region_ids = draw_region_ids(jax.random.fold_in(arg_keys[5], 71), 0)
    return {"e_start": e_start, "h_start": h_start, "inv_perm": inv_perm, "adj_seed": adj_seed, "region_ids": region_ids}


time_step = 0.5
grad_scale = 1.0 / 64.0

def neighbour(field_in, axis_pos, leading):
    widths = [(0, 0), (0, 0), (0, 0), (0, 0)]
    length = field_in.shape[axis_pos]
    if leading:
        widths[axis_pos] = (0, 1)
        padded = jnp.pad(field_in, widths)
        return lax.slice_in_dim(padded, 1, length + 1, axis=axis_pos)
    widths[axis_pos] = (1, 0)
    padded = jnp.pad(field_in, widths)
    return lax.slice_in_dim(padded, 0, length, axis=axis_pos)

def curl_of(field_in, leading):
    nearby = [neighbour(field_in, axis_pos, leading) for axis_pos in (1, 2, 3)]
    if leading:
        differences = [other - field_in for other in nearby]
    else:
        differences = [field_in - other for other in nearby]
    curl_first = differences[1][2] - differences[2][1]
    curl_second = differences[2][0] - differences[0][2]
    curl_third = differences[0][1] - differences[1][0]
    return jnp.stack([curl_first, curl_second, curl_third])

def reference(e_start, h_start, inv_perm, adj_seed, region_ids):

    def forward_run(perm_field):
        e_field, h_field = (e_start, h_start)
        for step_index in range(STEPS):
            h_field = h_field - time_step * curl_of(e_field, True)
            e_field = e_field + time_step * perm_field * curl_of(h_field, False)
        return e_field
    e_final, pullback = jax.vjp(forward_run, inv_perm)
    design_grad, = pullback(adj_seed)
    flat_grad = design_grad.reshape(3, -1).T
    sums = jax.ops.segment_sum(flat_grad, region_ids.reshape(-1).astype(jnp.int32), num_segments=REGIONS)
    return (e_final, sums.T * grad_scale)
```

```python
import functools

import jax
import jax.numpy as jnp
from jax import lax
from jax.experimental import pallas as pl
from jax.experimental.pallas import tpu as pltpu
from jax.sharding import PartitionSpec as P

STEPS = 4
REG_DEV = 8
DEEP = 4
EDGE = 4
UNROLL = 2

COUNTS = ((4, 4, 4), (3, 4, 4), (3, 3, 3), (3, 3, 3))
SLOTS = []
for _f in range(4):
    for _c in range(3):
        SLOTS.append((_f, _c, COUNTS[_f][_c], sum(s[2] for s in SLOTS)))
N_SLOTS = sum(s[2] for s in SLOTS)

grad_scale = 1.0 / 64.0
F32 = jnp.float32


def lanes_of(shape):
    return lax.broadcasted_iota(jnp.int32, shape, len(shape) - 1)


def rows_of(shape):
    return lax.broadcasted_iota(jnp.int32, shape, len(shape) - 2)


def pack_kernel(meta, e, h, ip, sd, a_out, b_out, z_out, y_out):
    even, gz = meta[0], meta[1]
    refs = (e, h, ip, sd)
    cx = e.shape[1]
    for f, c, k, off in SLOTS:
        top, bottom = cx - k, 0
        a_base = jnp.where(even == 1, top, bottom)
        b_base = jnp.where(even == 1, bottom, top)
        a_out[off : off + k] = refs[f][c, pl.ds(a_base, k)]
        b_out[off : off + k] = refs[f][c, pl.ds(b_base, k)]
    group = lanes_of((16, 128)) // EDGE
    z_off = jnp.where(gz == 0, EDGE, 0)
    for t in range(3):
        total = jnp.zeros((16, 128), F32)
        for k in range(4):
            f, c = divmod(4 * t + k, 3)
            for x in range(cx):
                moved = pltpu.roll(refs[f][c, x], (16 * x + 4 * k + z_off) % 128, 1)
                total = jnp.where(group == 4 * x + k, moved, total)
        z_out[t] = total
    first = rows_of((cx, 8, 128)) < EDGE
    for f in range(4):
        for c in range(3):
            q = 3 * f + c
            y_out[q * cx : (q + 1) * cx] = jnp.where(first, refs[f][c, :, 0:8], refs[f][c, :, 8:16])


def roll_up(v, axis):
    return pltpu.roll(v, v.shape[axis] - 1, axis)


def roll_down(v, axis):
    return pltpu.roll(v, 1, axis)


def curl_f(v, nxt, shift_y, shift_z):
    vx, vy, vz = v
    ny, nz = nxt
    return (
        (shift_y(vz) - vz) - (shift_z(vy) - vy),
        (shift_z(vx) - vx) - (nz - vz),
        (ny - vy) - (shift_y(vx) - vx),
    )


def curl_b(v, prv, shift_y, shift_z):
    vx, vy, vz = v
    py, pz = prv
    return (
        (vz - shift_y(vz)) - (vy - shift_z(vy)),
        (vx - shift_z(vx)) - (vz - pz),
        (vy - py) - (vx - shift_y(vx)),
    )


def run_kernel(meta, e_in, h_in, ip_in, sd_in, ids, a_in, b_in, z_in, za_in, zb_in, y1, y2,
               e_out, s_out, E, H, I, W, M, PS, G, SE, SH, SI, SW, SM, SP, SG):
    even, gz = meta[0], meta[1]
    low_x, keep_hi, keep_lo, low_y = meta[2], meta[3], meta[4], meta[5]
    first_owner, second_owner = meta[6], meta[7]
    cx = e_in.shape[1]
    shape = (24, 128)
    lane = lanes_of(shape)
    row = rows_of(shape)

    def y_part(v):
        r = rows_of(v.shape)
        keep = jnp.where(r < EDGE, keep_hi, keep_lo) == 1
        return jnp.where(keep, v, 0.0)

    ext = (E, H, I, PS.at[STEPS - 1])
    ins = (e_in, h_in, ip_in, sd_in)
    for f, c, k, off in SLOTS:
        X = ext[f]
        if k < DEEP:
            X[c, 0] = jnp.zeros(shape, F32)
            X[c, cx + 2 * DEEP - 1] = jnp.zeros(shape, F32)
        X[c, cx + 2 * DEEP] = jnp.zeros(shape, F32)
        q = 3 * f + c
        X[c, DEEP : DEEP + cx, 0:16] = ins[f][c]
        X[c, DEEP : DEEP + cx, 16:24] = y_part(y1[q * cx : (q + 1) * cx])
        a_base = jnp.where(even == 1, DEEP + cx, DEEP - k)
        b_base = jnp.where(even == 1, DEEP - k, DEEP + cx)
        X[c, pl.ds(a_base, k), 0:16] = a_in[off : off + k]
        X[c, pl.ds(a_base, k), 16:24] = y_part(y2[off : off + k])
        X[c, pl.ds(b_base, k), 0:16] = b_in[off : off + k]
        X[c, pl.ds(b_base, k), 16:24] = y_part(y2[N_SLOTS + off : N_SLOTS + off + k])

    zs = 2 * N_SLOTS
    is_even = even == 1
    own_off = jnp.where(gz == 0, 8, 4)
    own_j = jnp.where(gz == 0, 0, 4)
    got_j = jnp.where(gz == 0, 8, 0)
    j = lane % 16
    is_own = (j >= own_j) & (j < own_j + 8)
    is_got = (j >= got_j) & (j < got_j + EDGE)

    def with_y(ref, i, at):
        return jnp.concatenate([ref[i], y_part(y2[at])], axis=0)

    def strip_of(f, c, z_tiles):
        k = (3 * f + c) % 4
        tiles = []
        for t in range(2):
            acc = jnp.zeros(shape, F32)
            for x in range(8):
                moved = pltpu.roll(ext[f][c, 8 * t + x], (16 * x + own_off) % 128, 1)
                acc = jnp.where(lane // 16 == x, moved, acc)
            got = pltpu.roll(z_tiles[t], (got_j - 4 * k + 128) % 128, 1)
            tiles.append(jnp.where(is_own, acc, jnp.where(is_got, got, 0.0)))
        return jnp.concatenate(tiles, axis=1)

    strips = (SE, SH, SI, SP.at[STEPS - 1])
    for t in range(3):
        own = pltpu.roll(with_y(z_in, t, zs + t), 64, 1)
        from_a = pltpu.roll(with_y(za_in, t, zs + 3 + t), 64, 1)
        from_b = pltpu.roll(with_y(zb_in, t, zs + 6 + t), 64, 1)
        lower = jnp.where(is_even, from_b, from_a)
        upper = jnp.where(is_even, from_a, from_b)
        z_tiles = (jnp.where(lane < 64, lower, own), jnp.where(lane < 64, own, upper))
        for k in range(4):
            f, c = divmod(4 * t + k, 3)
            strips[f][c] = strip_of(f, c, z_tiles)

    def y_up(v):
        return roll_up(v, 0)

    def y_down(v):
        return roll_down(v, 0)

    def z_up(v):
        return jnp.where(lane == 127, 0.0, roll_up(v, 1))

    def z_down(v):
        return jnp.where(lane == 0, 0.0, roll_down(v, 1))

    def sz_up(v):
        return roll_up(v, 1)

    def sz_down(v):
        return roll_down(v, 1)

    def sx_up(v):
        return pltpu.roll(v, v.shape[1] - 16, 1)

    def sx_down(v):
        return pltpu.roll(v, 16, 1)

    keep_row = jnp.where((row >= 20) & (low_y == 0), 0.0, 1.0)
    s_shape = (24, 256)
    s_keep = jnp.where((rows_of(s_shape) >= 20) & (low_y == 0), 0.0, 1.0)
    s_keep = jnp.where((lanes_of(s_shape) < 16 * DEEP) & (low_x == 0), 0.0, s_keep)

    def keep_at(x):
        return keep_row * jnp.where((x < DEEP) & (low_x == 0), 0.0, 1.0)

    def sweep(lo, count, body):
        full, rest = divmod(count, UNROLL)

        def chunk(i, _):
            body([lo + i * UNROLL + u for u in range(UNROLL)])
            return 0

        lax.fori_loop(0, full, chunk, 0)
        if rest:
            body([lo + full * UNROLL + u for u in range(rest)])

    def get(ref, x, comps=(0, 1, 2)):
        return tuple(ref[c, x] for c in comps)

    def put(ref, xs, values):
        for x, v in zip(xs, values):
            for c in range(3):
                ref[c, x] = v[c]

    def sget(ref):
        return tuple(ref[c] for c in range(3))

    def sput(ref, v):
        for c in range(3):
            ref[c] = v[c]

    def scurl_f(v):
        return curl_f(v, (sx_up(v[1]), sx_up(v[2])), y_up, sz_up)

    def scurl_b(v):
        return curl_b(v, (sx_down(v[1]), sx_down(v[2])), y_down, sz_down)

    def halve(xs):
        new = []
        for x in xs:
            i, p = get(I, x), get(PS.at[STEPS - 1], x)
            half = tuple(0.5 * v for v in i)
            new.append((half, tuple(a * b for a, b in zip(half, p))))
        put(I, xs, [n[0] for n in new])
        put(W, xs, [n[1] for n in new])

    sweep(0, cx + 2 * DEEP, halve)
    half = tuple(0.5 * v for v in sget(SI))
    sput(SI, half)
    sput(SW, tuple(a * b for a, b in zip(half, sget(SP.at[STEPS - 1]))))

    last = cx + 2 * DEEP
    for m in range(STEPS - 1):
        n = STEPS - 1 - m

        def magnetic(xs, m=m):
            new = []
            for x in xs:
                curl = curl_f(get(W, x), get(W, x + 1, (1, 2)), y_up, z_up)
                keep = keep_at(x)
                if m == 0:
                    new.append(tuple(keep * v for v in curl))
                else:
                    new.append(tuple(q + keep * v for q, v in zip(get(M, x), curl)))
            put(M, xs, new)

        def electric(xs, m=m, n=n):
            new = []
            for x in xs:
                curl = curl_b(get(M, x), get(M, x - 1, (1, 2)), y_down, z_down)
                p = tuple(q - 0.5 * v for q, v in zip(get(PS.at[n], x), curl))
                new.append((p, tuple(a * b for a, b in zip(get(I, x), p))))
            put(PS.at[n - 1], xs, [v[0] for v in new])
            if m < STEPS - 2:
                put(W, xs, [v[1] for v in new])

        sweep(1 + m, last - 3 - 2 * m, magnetic)
        curl = scurl_f(sget(SW))
        if m == 0:
            merged = tuple(s_keep * v for v in curl)
        else:
            merged = tuple(q + s_keep * v for q, v in zip(sget(SM), curl))
        sput(SM, merged)
        p = tuple(q - 0.5 * v for q, v in zip(sget(SP.at[n]), scurl_b(merged)))
        sput(SP.at[n - 1], p)
        sput(SW, tuple(a * b for a, b in zip(sget(SI), p)))
        sweep(2 + m, last - 4 - 2 * m, electric)

    for n in range(STEPS):

        def magnetic(xs):
            new = []
            for x in xs:
                curl = curl_f(get(E, x), get(E, x + 1, (1, 2)), y_up, z_up)
                keep = 0.5 * keep_at(x)
                new.append(tuple(q - keep * v for q, v in zip(get(H, x), curl)))
            put(H, xs, new)

        def electric(xs, n=n):
            new = []
            for x in xs:
                curl = curl_b(get(H, x), get(H, x - 1, (1, 2)), y_down, z_down)
                e = tuple(q + i * v for q, i, v in zip(get(E, x), get(I, x), curl))
                g = tuple(p * v for p, v in zip(get(PS.at[n], x), curl))
                if n:
                    g = tuple(o + v for o, v in zip(get(G, x), g))
                new.append((e, g))
            put(E, xs, [v[0] for v in new])
            put(G, xs, [v[1] for v in new])

        sweep(n, last - 1 - 2 * n, magnetic)
        curl = scurl_f(sget(SE))
        sh = tuple(q - 0.5 * s_keep * v for q, v in zip(sget(SH), curl))
        sput(SH, sh)
        curl = scurl_b(sh)
        sput(SE, tuple(q + i * v for q, i, v in zip(sget(SE), sget(SI), curl)))
        g = tuple(p * v for p, v in zip(sget(SP.at[n]), curl))
        if n:
            g = tuple(o + v for o, v in zip(sget(SG), g))
        sput(SG, g)
        sweep(n + 1, last - 2 - 2 * n, electric)

    lane16 = lanes_of((16, 128))
    seam_lo = jnp.where(gz == 0, 128 - EDGE, 0)
    seam = (lane16 >= seam_lo) & (lane16 < seam_lo + EDGE)

    def merged_plane(main, strip, c, x):
        tile, at = divmod(x, 8)
        s = strip[c, 0:16, 128 * tile : 128 * (tile + 1)]
        moved = pltpu.roll(s, (seam_lo - 16 * at - EDGE + 256) % 128, 1)
        return jnp.where(seam, moved, main[c, x, 0:16])

    acc = jnp.zeros((80, 128), F32)
    for x in range(DEEP, DEEP + cx):
        grads = []
        for c in range(3):
            e_out[c, x - DEEP] = merged_plane(E, SE, c, x)
            grads.append(merged_plane(G, SG, c, x))
        lhs, rhs = [], []
        for r in range(2):
            g = jnp.concatenate([v[8 * r : 8 * r + 8] for v in grads], axis=0)
            one = g.astype(jnp.bfloat16).astype(F32)
            rest = g - one
            two = rest.astype(jnp.bfloat16).astype(F32)
            three = rest - two
            lhs.append(jnp.concatenate([one, two, three, jnp.zeros((8, 128), F32)], axis=0).astype(jnp.bfloat16))
            region = ids[x - DEEP, 8 * r : 8 * r + 8]
            slot = jnp.where(
                region < second_owner * REG_DEV,
                region - first_owner * REG_DEV,
                region - second_owner * REG_DEV + REG_DEV,
            )
            hot = jnp.concatenate([jnp.where(slot == s, 1.0, 0.0) for s in range(2 * REG_DEV)], axis=0)
            rhs.append(hot.astype(jnp.bfloat16))
        acc = acc + lax.dot_general(
            jnp.concatenate(lhs, axis=1),
            jnp.concatenate(rhs, axis=1),
            (((1,), (1,)), ((), ())),
            preferred_element_type=F32,
        )
    sums = acc[0:24] + acc[24:48] + acc[48:72]
    sums = jnp.where(rows_of((24, 128)) % 8 == lanes_of((24, 128)) % 8, sums, 0.0)
    parts = [jnp.sum(sums[8 * c : 8 * c + 8], axis=0, keepdims=True) for c in range(3)]
    parts = jnp.concatenate(parts + [jnp.zeros((5, 128), F32)], axis=0)
    fold = jnp.where(rows_of((128, 128)) // 8 == lanes_of((128, 128)), 0.5 * grad_scale, 0.0)
    s_out[...] = jnp.dot(parts, fold, precision=lax.Precision.HIGHEST, preferred_element_type=F32)


def y_rows(v):
    first = lax.broadcasted_iota(jnp.int32, (1, 8, 1), 1) < EDGE
    return jnp.where(first, v[:, 0:8], v[:, 8:16])


def local(e_start, h_start, inv_perm, adj_seed, region_ids):
    n_gx, n_gy, n_gz = (lax.axis_size(a) for a in ("gx", "gy", "gz"))
    xi, yi, zi = (lax.axis_index(a) for a in ("gx", "gy", "gz"))
    cx = e_start.shape[1]
    even = (xi + 1) % 2
    plane_count = n_gy * n_gz
    own_flat = xi * plane_count + yi * n_gz + zi
    first_owner = own_flat - (1 - even) * plane_count
    keep_hi = jnp.where(yi < n_gy - 1, 1, 0)
    keep_lo = jnp.where(yi > 0, 1, 0)
    meta = jnp.stack(
        [even, zi, jnp.where(xi > 0, 1, 0), keep_hi, keep_lo, keep_lo, first_owner, first_owner + plane_count]
    ).astype(jnp.int32)
    smem = pl.BlockSpec(memory_space=pltpu.SMEM)
    vmem = pl.BlockSpec(memory_space=pltpu.VMEM)
    shape = lambda *dims: jax.ShapeDtypeStruct(dims, F32)

    a_pairs = [(i, i ^ 1) for i in range(n_gx)]
    b_pairs = [(i, ((i - 1) ^ 1) + 1) for i in range(1, n_gx - 1)]

    def swap_y(v):
        if n_gy == 2:
            return lax.ppermute(v, "gy", [(0, 1), (1, 0)])
        up = lax.ppermute(v, "gy", [(i, i + 1) for i in range(n_gy - 1)])
        down = lax.ppermute(v, "gy", [(i + 1, i) for i in range(n_gy - 1)])
        first = lax.broadcasted_iota(jnp.int32, (1, 8, 1), 1) < EDGE
        return jnp.where(first, down, up)

    a_msg, b_msg, z_msg, y_msg = pl.pallas_call(
        pack_kernel,
        out_shape=(shape(N_SLOTS, 16, 128), shape(N_SLOTS, 16, 128), shape(3, 16, 128), shape(12 * cx, 8, 128)),
        in_specs=[smem] + [vmem] * 4,
        out_specs=(vmem,) * 4,
    )(meta, e_start, h_start, inv_perm, adj_seed)

    a_got = lax.ppermute(a_msg, "gx", a_pairs)
    b_got = lax.ppermute(b_msg, "gx", b_pairs)
    z_got = lax.ppermute(z_msg, "gz", [(0, 1), (1, 0)])
    y1 = swap_y(y_msg)
    za_got = lax.ppermute(z_got, "gx", a_pairs)
    zb_got = lax.ppermute(z_got, "gx", b_pairs)
    y2 = swap_y(jnp.concatenate([y_rows(v) for v in (a_got, b_got, z_got, za_got, zb_got)], axis=0))

    planes = cx + 2 * DEEP + 1
    main = pltpu.VMEM((3, planes, 24, 128), F32)
    strip = pltpu.VMEM((3, 24, 256), F32)
    e_field, sums = pl.pallas_call(
        run_kernel,
        out_shape=(shape(*e_start.shape), shape(8, 128)),
        in_specs=[smem] + [vmem] * 12,
        out_specs=(vmem, vmem),
        scratch_shapes=[main] * 5
        + [pltpu.VMEM((STEPS, 3, planes, 24, 128), F32), main]
        + [strip] * 5
        + [pltpu.VMEM((STEPS, 3, 24, 256), F32), strip],
        compiler_params=pltpu.CompilerParams(vmem_limit_bytes=40 * 1024 * 1024),
    )(meta, e_start, h_start, inv_perm, adj_seed, region_ids, a_got, b_got, z_got, za_got, zb_got, y1, y2)

    total = sums + lax.ppermute(sums, "gx", a_pairs)
    owned = jnp.where(even == 1, total[0:3, 0:REG_DEV], total[0:3, REG_DEV : 2 * REG_DEV])
    return e_field, owned


def solution(mesh):
    placed = (
        P(None, "gx", "gy", "gz"),
        P(None, "gx", "gy", "gz"),
        P(None, "gx", "gy", "gz"),
        P(None, "gx", "gy", "gz"),
        P("gx", "gy", "gz"),
    )
    return jax.shard_map(
        local,
        mesh=mesh,
        in_specs=placed,
        out_specs=(P(None, "gx", "gy", "gz"), P(None, ("gx", "gy", "gz"))),
        check_vma=False,
    )
```

```python
import jax
import jax.numpy as jnp
from jax import lax
from jax.experimental import pallas as pl
from jax.experimental.pallas import tpu as pltpu
from jax.sharding import PartitionSpec as P

STEPS = 4
REG_DEV = 8
DEEP = 4
EDGE = 4
UNROLL = 8

COUNTS = ((4, 4, 4), (3, 4, 4), (3, 3, 3), (3, 3, 3))
SLOTS = []
for _f in range(4):
    for _c in range(3):
        SLOTS.append((_f, _c, COUNTS[_f][_c], sum(s[2] for s in SLOTS)))
N_SLOTS = sum(s[2] for s in SLOTS)

grad_scale = 1.0 / 64.0
F32 = jnp.float32


def lanes_of(shape):
    return lax.broadcasted_iota(jnp.int32, shape, len(shape) - 1)


def rows_of(shape):
    return lax.broadcasted_iota(jnp.int32, shape, len(shape) - 2)


def pack_kernel(e, h, ip, sd, a_out, b_out, z_out, y_out):
    even, gz = (lax.axis_index("gx") + 1) % 2, lax.axis_index("gz")
    refs = (e, h, ip, sd)
    cx = e.shape[1]
    for f, c, k, off in SLOTS:
        top, bottom = cx - k, 0
        a_base = jnp.where(even == 1, top, bottom)
        b_base = jnp.where(even == 1, bottom, top)
        a_out[off : off + k] = refs[f][c, pl.ds(a_base, k)]
        b_out[off : off + k] = refs[f][c, pl.ds(b_base, k)]
    group = lanes_of((16, 128)) // EDGE
    z_off = jnp.where(gz == 0, EDGE, 0)
    for t in range(3):
        total = jnp.zeros((16, 128), F32)
        for k in range(4):
            f, c = divmod(4 * t + k, 3)
            for x in range(cx):
                moved = pltpu.roll(refs[f][c, x], (16 * x + 4 * k + z_off) % 128, 1)
                total = jnp.where(group == 4 * x + k, moved, total)
        z_out[t] = total
    first = rows_of((cx, 8, 128)) < EDGE
    for f in range(4):
        for c in range(3):
            q = 3 * f + c
            y_out[q * cx : (q + 1) * cx] = jnp.where(first, refs[f][c, :, 0:8], refs[f][c, :, 8:16])


def roll_up(v, axis):
    return pltpu.roll(v, v.shape[axis] - 1, axis)


def roll_down(v, axis):
    return pltpu.roll(v, 1, axis)


def curl_f(v, nxt, shift_y, shift_z):
    vx, vy, vz = v
    ny, nz = nxt
    return (
        (shift_y(vz) - vz) - (shift_z(vy) - vy),
        (shift_z(vx) - vx) - (nz - vz),
        (ny - vy) - (shift_y(vx) - vx),
    )


def curl_b(v, prv, shift_y, shift_z):
    vx, vy, vz = v
    py, pz = prv
    return (
        (vz - shift_y(vz)) - (vy - shift_z(vy)),
        (vx - shift_z(vx)) - (vz - pz),
        (vy - py) - (vx - shift_y(vx)),
    )


def run_kernel(e_in, h_in, ip_in, sd_in, ids, a_in, b_in, z_in, za_in, zb_in, y1, y2,
               e_out, s_out, E, H, I, W, M, PS, G, SE, SH, SI, SW, SM, SP, SG):
    xi, yi, gz = (lax.axis_index(a) for a in ("gx", "gy", "gz"))
    even = (xi + 1) % 2
    low_x = jnp.where(xi > 0, 1, 0)
    keep_hi = jnp.where(yi < lax.axis_size("gy") - 1, 1, 0)
    keep_lo = low_y = jnp.where(yi > 0, 1, 0)
    plane_count = lax.axis_size("gy") * lax.axis_size("gz")
    own_flat = xi * plane_count + yi * lax.axis_size("gz") + gz
    first_owner = own_flat - (1 - even) * plane_count
    second_owner = first_owner + plane_count
    cx = e_in.shape[1]
    shape = (24, 128)
    lane = lanes_of(shape)
    row = rows_of(shape)

    def y_part(v):
        r = rows_of(v.shape)
        keep = jnp.where(r < EDGE, keep_hi, keep_lo) == 1
        return jnp.where(keep, v, 0.0)

    ext = (E, H, I, PS.at[STEPS - 1])
    ins = (e_in, h_in, ip_in, sd_in)
    for f, c, k, off in SLOTS:
        X = ext[f]
        if k < DEEP:
            X[c, 0] = jnp.zeros(shape, F32)
            X[c, cx + 2 * DEEP - 1] = jnp.zeros(shape, F32)
        X[c, cx + 2 * DEEP] = jnp.zeros(shape, F32)
        q = 3 * f + c
        X[c, DEEP : DEEP + cx, 0:16] = ins[f][c]
        X[c, DEEP : DEEP + cx, 16:24] = y_part(y1[q * cx : (q + 1) * cx])
        a_base = jnp.where(even == 1, DEEP + cx, DEEP - k)
        b_base = jnp.where(even == 1, DEEP - k, DEEP + cx)
        X[c, pl.ds(a_base, k), 0:16] = a_in[off : off + k]
        X[c, pl.ds(a_base, k), 16:24] = y_part(y2[off : off + k])
        X[c, pl.ds(b_base, k), 0:16] = b_in[off : off + k]
        X[c, pl.ds(b_base, k), 16:24] = y_part(y2[N_SLOTS + off : N_SLOTS + off + k])

    zs = 2 * N_SLOTS
    is_even = even == 1
    own_off = jnp.where(gz == 0, 8, 4)
    own_j = jnp.where(gz == 0, 0, 4)
    got_j = jnp.where(gz == 0, 8, 0)
    j = lane % 16
    is_own = (j >= own_j) & (j < own_j + 8)
    is_got = (j >= got_j) & (j < got_j + EDGE)

    def with_y(ref, i, at):
        return jnp.concatenate([ref[i], y_part(y2[at])], axis=0)

    def strip_of(f, c, z_tiles):
        k = (3 * f + c) % 4
        tiles = []
        for t in range(2):
            acc = jnp.zeros(shape, F32)
            for x in range(8):
                moved = pltpu.roll(ext[f][c, 8 * t + x], (16 * x + own_off) % 128, 1)
                acc = jnp.where(lane // 16 == x, moved, acc)
            got = pltpu.roll(z_tiles[t], (got_j - 4 * k + 128) % 128, 1)
            tiles.append(jnp.where(is_own, acc, jnp.where(is_got, got, 0.0)))
        return jnp.concatenate(tiles, axis=1)

    strips = (SE, SH, SI, SP.at[STEPS - 1])
    for t in range(3):
        own = pltpu.roll(with_y(z_in, t, zs + t), 64, 1)
        from_a = pltpu.roll(with_y(za_in, t, zs + 3 + t), 64, 1)
        from_b = pltpu.roll(with_y(zb_in, t, zs + 6 + t), 64, 1)
        lower = jnp.where(is_even, from_b, from_a)
        upper = jnp.where(is_even, from_a, from_b)
        z_tiles = (jnp.where(lane < 64, lower, own), jnp.where(lane < 64, own, upper))
        for k in range(4):
            f, c = divmod(4 * t + k, 3)
            strips[f][c] = strip_of(f, c, z_tiles)

    def y_up(v):
        return roll_up(v, 0)

    def y_down(v):
        return roll_down(v, 0)

    def z_up(v):
        return jnp.where(lane == 127, 0.0, roll_up(v, 1))

    def z_down(v):
        return jnp.where(lane == 0, 0.0, roll_down(v, 1))

    def sz_up(v):
        return roll_up(v, 1)

    def sz_down(v):
        return roll_down(v, 1)

    def sx_up(v):
        return pltpu.roll(v, v.shape[1] - 16, 1)

    def sx_down(v):
        return pltpu.roll(v, 16, 1)

    keep_row = jnp.where((row >= 20) & (low_y == 0), 0.0, 1.0)
    s_shape = (24, 256)
    s_keep = jnp.where((rows_of(s_shape) >= 20) & (low_y == 0), 0.0, 1.0)
    s_keep = jnp.where((lanes_of(s_shape) < 16 * DEEP) & (low_x == 0), 0.0, s_keep)

    def keep_at(x):
        return keep_row * jnp.where((x < DEEP) & (low_x == 0), 0.0, 1.0)

    def sweep(lo, count, body):
        full, rest = divmod(count, UNROLL)

        def chunk(i, _):
            body([lo + i * UNROLL + u for u in range(UNROLL)])
            return 0

        lax.fori_loop(0, full, chunk, 0)
        if rest:
            body([lo + full * UNROLL + u for u in range(rest)])

    def get(ref, x, comps=(0, 1, 2)):
        return tuple(ref[c, x] for c in comps)

    def put(ref, xs, values):
        for x, v in zip(xs, values):
            for c in range(3):
                ref[c, x] = v[c]

    def sget(ref):
        return tuple(ref[c] for c in range(3))

    def sput(ref, v):
        for c in range(3):
            ref[c] = v[c]

    def scurl_f(v):
        return curl_f(v, (sx_up(v[1]), sx_up(v[2])), y_up, sz_up)

    def scurl_b(v):
        return curl_b(v, (sx_down(v[1]), sx_down(v[2])), y_down, sz_down)

    def halve(xs):
        new = []
        for x in xs:
            i, p = get(I, x), get(PS.at[STEPS - 1], x)
            half = tuple(0.5 * v for v in i)
            new.append((half, tuple(a * b for a, b in zip(half, p))))
        put(I, xs, [n[0] for n in new])
        put(W, xs, [n[1] for n in new])

    sweep(0, cx + 2 * DEEP, halve)
    half = tuple(0.5 * v for v in sget(SI))
    sput(SI, half)
    sput(SW, tuple(a * b for a, b in zip(half, sget(SP.at[STEPS - 1]))))

    last = cx + 2 * DEEP
    for m in range(STEPS - 1):
        n = STEPS - 1 - m

        def magnetic(xs, m=m):
            new = []
            for x in xs:
                curl = curl_f(get(W, x), get(W, x + 1, (1, 2)), y_up, z_up)
                keep = keep_at(x)
                if m == 0:
                    new.append(tuple(keep * v for v in curl))
                else:
                    new.append(tuple(q + keep * v for q, v in zip(get(M, x), curl)))
            put(M, xs, new)

        def electric(xs, m=m, n=n):
            new = []
            for x in xs:
                curl = curl_b(get(M, x), get(M, x - 1, (1, 2)), y_down, z_down)
                p = tuple(q - 0.5 * v for q, v in zip(get(PS.at[n], x), curl))
                new.append((p, tuple(a * b for a, b in zip(get(I, x), p))))
            put(PS.at[n - 1], xs, [v[0] for v in new])
            if m < STEPS - 2:
                put(W, xs, [v[1] for v in new])

        sweep(1 + m, last - 3 - 2 * m, magnetic)
        curl = scurl_f(sget(SW))
        if m == 0:
            merged = tuple(s_keep * v for v in curl)
        else:
            merged = tuple(q + s_keep * v for q, v in zip(sget(SM), curl))
        sput(SM, merged)
        p = tuple(q - 0.5 * v for q, v in zip(sget(SP.at[n]), scurl_b(merged)))
        sput(SP.at[n - 1], p)
        sput(SW, tuple(a * b for a, b in zip(sget(SI), p)))
        sweep(2 + m, last - 4 - 2 * m, electric)

    for n in range(STEPS):

        def magnetic(xs):
            new = []
            for x in xs:
                curl = curl_f(get(E, x), get(E, x + 1, (1, 2)), y_up, z_up)
                keep = 0.5 * keep_at(x)
                new.append(tuple(q - keep * v for q, v in zip(get(H, x), curl)))
            put(H, xs, new)

        def electric(xs, n=n):
            new = []
            for x in xs:
                curl = curl_b(get(H, x), get(H, x - 1, (1, 2)), y_down, z_down)
                e = tuple(q + i * v for q, i, v in zip(get(E, x), get(I, x), curl))
                g = tuple(p * v for p, v in zip(get(PS.at[n], x), curl))
                if n:
                    g = tuple(o + v for o, v in zip(get(G, x), g))
                new.append((e, g))
            put(E, xs, [v[0] for v in new])
            put(G, xs, [v[1] for v in new])

        sweep(n, last - 1 - 2 * n, magnetic)
        curl = scurl_f(sget(SE))
        sh = tuple(q - 0.5 * s_keep * v for q, v in zip(sget(SH), curl))
        sput(SH, sh)
        curl = scurl_b(sh)
        sput(SE, tuple(q + i * v for q, i, v in zip(sget(SE), sget(SI), curl)))
        g = tuple(p * v for p, v in zip(sget(SP.at[n]), curl))
        if n:
            g = tuple(o + v for o, v in zip(sget(SG), g))
        sput(SG, g)
        sweep(n + 1, last - 2 - 2 * n, electric)

    lane16 = lanes_of((16, 128))
    seam_lo = jnp.where(gz == 0, 128 - EDGE, 0)
    seam = (lane16 >= seam_lo) & (lane16 < seam_lo + EDGE)

    def merged_plane(main, strip, c, x):
        tile, at = divmod(x, 8)
        s = strip[c, 0:16, 128 * tile : 128 * (tile + 1)]
        moved = pltpu.roll(s, (seam_lo - 16 * at - EDGE + 256) % 128, 1)
        return jnp.where(seam, moved, main[c, x, 0:16])

    acc = jnp.zeros((80, 128), F32)
    for x in range(DEEP, DEEP + cx):
        grads = []
        for c in range(3):
            e_out[c, x - DEEP] = merged_plane(E, SE, c, x)
            grads.append(merged_plane(G, SG, c, x))
        lhs, rhs = [], []
        for r in range(2):
            g = jnp.concatenate([v[8 * r : 8 * r + 8] for v in grads], axis=0)
            one = g.astype(jnp.bfloat16).astype(F32)
            rest = g - one
            two = rest.astype(jnp.bfloat16).astype(F32)
            three = rest - two
            lhs.append(jnp.concatenate([one, two, three, jnp.zeros((8, 128), F32)], axis=0).astype(jnp.bfloat16))
            region = ids[x - DEEP, 8 * r : 8 * r + 8]
            slot = jnp.where(
                region < second_owner * REG_DEV,
                region - first_owner * REG_DEV,
                region - second_owner * REG_DEV + REG_DEV,
            )
            hot = jnp.concatenate([jnp.where(slot == s, 1.0, 0.0) for s in range(2 * REG_DEV)], axis=0)
            rhs.append(hot.astype(jnp.bfloat16))
        acc = acc + lax.dot_general(
            jnp.concatenate(lhs, axis=1),
            jnp.concatenate(rhs, axis=1),
            (((1,), (1,)), ((), ())),
            preferred_element_type=F32,
        )
    sums = acc[0:24] + acc[24:48] + acc[48:72]
    sums = jnp.where(rows_of((24, 128)) % 8 == lanes_of((24, 128)) % 8, sums, 0.0)
    parts = [jnp.sum(sums[8 * c : 8 * c + 8], axis=0, keepdims=True) for c in range(3)]
    parts = jnp.concatenate(parts + [jnp.zeros((5, 128), F32)], axis=0)
    fold = jnp.where(rows_of((128, 128)) // 8 == lanes_of((128, 128)), 0.5 * grad_scale, 0.0)
    s_out[...] = jnp.dot(parts, fold, precision=lax.Precision.HIGHEST, preferred_element_type=F32)


def y_rows(v):
    first = lax.broadcasted_iota(jnp.int32, (1, 8, 1), 1) < EDGE
    return jnp.where(first, v[:, 0:8], v[:, 8:16])


def local(e_start, h_start, inv_perm, adj_seed, region_ids):
    n_gx, n_gy = lax.axis_size("gx"), lax.axis_size("gy")
    xi = lax.axis_index("gx")
    cx = e_start.shape[1]
    even = (xi + 1) % 2
    vmem = pl.BlockSpec(memory_space=pltpu.VMEM)
    shape = lambda *dims: jax.ShapeDtypeStruct(dims, F32)

    a_pairs = [(i, i ^ 1) for i in range(n_gx)]
    b_pairs = [(i, ((i - 1) ^ 1) + 1) for i in range(1, n_gx - 1)]

    def swap_y(v):
        if n_gy == 2:
            return lax.ppermute(v, "gy", [(0, 1), (1, 0)])
        up = lax.ppermute(v, "gy", [(i, i + 1) for i in range(n_gy - 1)])
        down = lax.ppermute(v, "gy", [(i + 1, i) for i in range(n_gy - 1)])
        first = lax.broadcasted_iota(jnp.int32, (1, 8, 1), 1) < EDGE
        return jnp.where(first, down, up)

    a_msg, b_msg, z_msg, y_msg = pl.pallas_call(
        pack_kernel,
        out_shape=(shape(N_SLOTS, 16, 128), shape(N_SLOTS, 16, 128), shape(3, 16, 128), shape(12 * cx, 8, 128)),
        in_specs=[vmem] * 4,
        out_specs=(vmem,) * 4,
        compiler_params=pltpu.CompilerParams(vmem_limit_bytes=8 * 1024 * 1024),
    )(e_start, h_start, inv_perm, adj_seed)

    a_got = lax.ppermute(a_msg, "gx", a_pairs)
    b_got = lax.ppermute(b_msg, "gx", b_pairs)
    z_got = lax.ppermute(z_msg, "gz", [(0, 1), (1, 0)])
    y1 = swap_y(y_msg)
    za_got = lax.ppermute(z_got, "gx", a_pairs)
    zb_got = lax.ppermute(z_got, "gx", b_pairs)
    y2 = swap_y(jnp.concatenate([y_rows(v) for v in (a_got, b_got, z_got, za_got, zb_got)], axis=0))

    planes = cx + 2 * DEEP + 1
    main = pltpu.VMEM((3, planes, 24, 128), F32)
    strip = pltpu.VMEM((3, 24, 256), F32)
    e_field, sums = pl.pallas_call(
        run_kernel,
        out_shape=(shape(*e_start.shape), shape(8, 128)),
        in_specs=[vmem] * 12,
        out_specs=(vmem, vmem),
        scratch_shapes=[main] * 5
        + [pltpu.VMEM((STEPS, 3, planes, 24, 128), F32), main]
        + [strip] * 5
        + [pltpu.VMEM((STEPS, 3, 24, 256), F32), strip],
        compiler_params=pltpu.CompilerParams(vmem_limit_bytes=20 * 1024 * 1024),
    )(e_start, h_start, inv_perm, adj_seed, region_ids, a_got, b_got, z_got, za_got, zb_got, y1, y2)

    total = sums + lax.ppermute(sums, "gx", a_pairs)
    owned = jnp.where(even == 1, total[0:3, 0:REG_DEV], total[0:3, REG_DEV : 2 * REG_DEV])
    return e_field, owned


def solution(mesh):
    placed = (
        P(None, "gx", "gy", "gz"),
        P(None, "gx", "gy", "gz"),
        P(None, "gx", "gy", "gz"),
        P(None, "gx", "gy", "gz"),
        P("gx", "gy", "gz"),
    )
    return jax.shard_map(
        local,
        mesh=mesh,
        in_specs=placed,
        out_specs=(P(None, "gx", "gy", "gz"), P(None, ("gx", "gy", "gz"))),
        check_vma=False,
    )
```

```python
import jax
import jax.numpy as jnp
from jax import lax
from jax.experimental import pallas as pl
from jax.experimental.pallas import tpu as pltpu
from jax.sharding import PartitionSpec as P

STEPS = 4
REG_DEV = 8
DEEP = 3
EDGE = 4
PERM, SEED, ELEC, MAGN = range(4)
N_SLOTS = 2 * 3 * DEEP
N_TRACES = 2 * STEPS

time_step = 0.5
grad_scale = 1.0 / 64.0
F32 = jnp.float32


def lanes_of(shape):
    return lax.broadcasted_iota(jnp.int32, shape, len(shape) - 1)


def rows_of(shape):
    return lax.broadcasted_iota(jnp.int32, shape, len(shape) - 2)


def roll_up(v, axis):
    return pltpu.roll(v, v.shape[axis] - 1, axis)


def roll_down(v, axis):
    return pltpu.roll(v, 1, axis)


def curl_f(v, nxt, shift_y, shift_z):
    vx, vy, vz = v
    ny, nz = nxt
    return (
        (shift_y(vz) - vz) - (shift_z(vy) - vy),
        (shift_z(vx) - vx) - (nz - vz),
        (ny - vy) - (shift_y(vx) - vx),
    )


def curl_b(v, prv, shift_y, shift_z):
    vx, vy, vz = v
    py, pz = prv
    return (
        (vz - shift_y(vz)) - (vy - shift_z(vy)),
        (vx - shift_z(vx)) - (vz - pz),
        (vy - py) - (vx - shift_y(vx)),
    )


class Place:
    def __init__(self):
        xi, yi, self.gz = (lax.axis_index(a) for a in ("gx", "gy", "gz"))
        n_gy, n_gz = lax.axis_size("gy"), lax.axis_size("gz")
        even = (xi + 1) % 2
        self.even = even == 1
        self.no_low_x = xi == 0
        self.no_low_y = yi == 0
        self.no_high_y = yi == n_gy - 1
        own_flat = xi * n_gy * n_gz + yi * n_gz + self.gz
        self.first_owner = own_flat - (1 - even) * n_gy * n_gz
        self.second_owner = self.first_owner + n_gy * n_gz
        self.lane = lanes_of((24, 128))
        self.row = rows_of((24, 128))
        self.keep_row = jnp.where((self.row >= 20) & self.no_low_y, 0.0, 1.0)
        self.own_off = jnp.where(self.gz == 0, 8, 4)
        self.own_j = jnp.where(self.gz == 0, 0, 4)
        self.got_j = jnp.where(self.gz == 0, 8, 0)

    def y_part(self, v):
        high = jnp.where(self.no_high_y, 0.0, 1.0)
        low = jnp.where(self.no_low_y, 0.0, 1.0)
        return v * jnp.where(rows_of(v.shape[-2:]) < EDGE, high, low)

    def strip_tile(self, planes, got, q):
        lane = self.lane
        acc = jnp.zeros((24, 128), F32)
        for x, plane in enumerate(planes):
            acc = jnp.where(lane // 16 == x, pltpu.roll(plane, (16 * x + self.own_off) % 128, 1), acc)
        j = lane % 16
        is_own = (j >= self.own_j) & (j < self.own_j + 8)
        is_got = (j >= self.got_j) & (j < self.got_j + EDGE)
        got = pltpu.roll(got, (self.got_j - 4 * (q % 4) + 128) % 128, 1)
        return jnp.where(is_own, acc, jnp.where(is_got, got, 0.0))

    def z_up(self, v):
        return jnp.where(self.lane == 127, 0.0, roll_up(v, 1))

    def z_down(self, v):
        return jnp.where(self.lane == 0, 0.0, roll_down(v, 1))


def y_up(v):
    return roll_up(v, 0)


def y_down(v):
    return roll_down(v, 0)


def sz_up(v):
    return roll_up(v, 1)


def sz_down(v):
    return roll_down(v, 1)


def get(ref, x, comps=(0, 1, 2)):
    return tuple(ref[c, x] for c in comps)


def put(ref, xs, values):
    for x, v in zip(xs, values):
        for c in range(3):
            ref[c, x] = v[c]


def sget(ref):
    return tuple(ref[c] for c in range(3))


def sput(ref, v):
    for c in range(3):
        ref[c] = v[c]


def pack_kernel(ip_hbm, sd_hbm, e_hbm, h_hbm, a_out, b_out, z_out, y_out, ip, sd, e, h, sems):
    even, gz = (lax.axis_index("gx") + 1) % 2, lax.axis_index("gz")
    refs = (ip, sd, e, h)
    copies = []
    for i, src in enumerate((ip_hbm, sd_hbm, e_hbm, h_hbm)):
        copies.append(pltpu.make_async_copy(src, refs[i], sems.at[i]))
    for copy in copies:
        copy.start()
    for copy in copies:
        copy.wait()
    cx = e.shape[1]
    a_base = jnp.where(even == 1, cx - DEEP, 0)
    b_base = jnp.where(even == 1, 0, cx - DEEP)
    for f in (PERM, SEED):
        for c in range(3):
            off = DEEP * (3 * f + c)
            a_out[off : off + DEEP] = refs[f][c, pl.ds(a_base, DEEP)]
            b_out[off : off + DEEP] = refs[f][c, pl.ds(b_base, DEEP)]
    group = lanes_of((16, 128)) // EDGE
    z_off = jnp.where(gz == 0, EDGE, 0)
    for t in range(3):
        total = jnp.zeros((16, 128), F32)
        for k in range(4):
            f, c = divmod(4 * t + k, 3)
            for x in range(cx):
                moved = pltpu.roll(refs[f][c, x], (16 * x + 4 * k + z_off) % 128, 1)
                total = jnp.where(group == 4 * x + k, moved, total)
        z_out[t] = total
    first = rows_of((cx, 8, 128)) < EDGE
    for f in range(4):
        for c in range(3):
            q = 3 * f + c
            y_out[q * cx : (q + 1) * cx] = jnp.where(first, refs[f][c, :, 0:8], refs[f][c, :, 8:16])


def own_kernel(ip_in, e_in, h_in, y1, z_in, yz,
               a_out, b_out, c_out, e_out, sc_out, se_out, I, E, H):
    at = Place()
    cx = e_in.shape[1]
    lane = at.lane
    zero = jnp.zeros((24, 128), F32)
    strips = []
    for f, X, src in ((PERM, I, ip_in), (ELEC, E, e_in), (MAGN, H, h_in)):
        strip = []
        for c in range(3):
            q = 3 * f + c
            X[c, 0] = zero
            X[c, cx + 1] = zero
            X[c, 1 : cx + 1, 0:16] = src[c]
            X[c, 1 : cx + 1, 16:24] = at.y_part(y1[q * cx : (q + 1) * cx])
            if f == PERM:
                X[c] = time_step * X[c]
            got = jnp.concatenate([z_in[q // 4], at.y_part(yz[q // 4])], axis=0)
            tile = at.strip_tile([X[c, x] for x in range(1, cx + 1)], time_step * got if f == PERM else got, q)
            strip.append(tile)
        strips.append(tuple(strip))
    si, se, sh = strips

    def sx_up(v):
        return jnp.where(lane >= 112, 0.0, pltpu.roll(v, 112, 1))

    def sx_down(v):
        return jnp.where(lane < 16, 0.0, pltpu.roll(v, 16, 1))

    xs = list(range(1, cx + 1))
    up_strip, down_strip = zero, zero
    for n in range(STEPS):
        downs = get(E, 1, (1, 2))
        new = []
        for x in xs:
            curl = curl_f(get(E, x), get(E, x + 1, (1, 2)), y_up, at.z_up)
            keep = time_step * at.keep_row
            new.append(tuple(q - keep * v for q, v in zip(get(H, x), curl)))
        put(H, xs, new)
        curl = curl_f(se, (sx_up(se[1]), sx_up(se[2])), y_up, sz_up)
        down_from = se
        sh = tuple(q - time_step * at.keep_row * v for q, v in zip(sh, curl))
        ups = get(H, cx, (1, 2))
        new, curls = [], []
        for x in xs:
            curl = curl_b(get(H, x), get(H, x - 1, (1, 2)), y_down, at.z_down)
            new.append(tuple(q + i * v for q, i, v in zip(get(E, x), get(I, x), curl)))
            curls.append(curl)
        put(E, xs, new)
        for x, curl in zip(xs, curls):
            for c in range(3):
                c_out[n, c, x - 1] = curl[c][0:16]
        curl = curl_b(sh, (sx_down(sh[1]), sx_down(sh[2])), y_down, sz_down)
        se = tuple(q + i * v for q, i, v in zip(se, si, curl))
        for c in range(3):
            sc_out[n, c] = curl[c]
        for k in range(2):
            i = 2 * n + k
            a_out[i] = jnp.where(at.even, ups[k], downs[k])
            b_out[i] = jnp.where(at.even, downs[k], ups[k])
            here = lane // 16 == i
            up_strip = jnp.where(here, pltpu.roll(sh[1 + k], (16 * i + 16) % 128, 1), up_strip)
            down_strip = jnp.where(here, pltpu.roll(down_from[1 + k], 16 * i, 1), down_strip)
    a_out[N_TRACES] = jnp.where(at.even, up_strip, down_strip)
    b_out[N_TRACES] = jnp.where(at.even, down_strip, up_strip)
    for c in range(3):
        e_out[c] = E[c, 1 : cx + 1, 0:16]
    sput(se_out, se)


def adjoint_kernel(ip_in, sd_in, a_in, b_in, z_in, za_in, zb_in, y1, yz, y2, c_own, sc_own,
                   i_out, si_out, p_out, sp_out, g_out, sg_out, I, W, M, PS, SI, SW, SM, SP):
    at = Place()
    cx = ip_in.shape[1]
    lane = at.lane
    last = cx + 2 * DEEP
    top = STEPS - 1
    a_base = jnp.where(at.even, DEEP + cx, 0)
    b_base = jnp.where(at.even, 0, DEEP + cx)
    for f, X, src in ((PERM, I, ip_in), (SEED, PS.at[top], sd_in)):
        for c in range(3):
            q = 3 * f + c
            off = DEEP * q
            X[c, last] = jnp.zeros((24, 128), F32)
            X[c, DEEP : DEEP + cx, 0:16] = src[c]
            X[c, DEEP : DEEP + cx, 16:24] = at.y_part(y1[q * cx : (q + 1) * cx])
            X[c, pl.ds(a_base, DEEP), 0:16] = a_in[off : off + DEEP]
            X[c, pl.ds(a_base, DEEP), 16:24] = at.y_part(y2[off : off + DEEP])
            X[c, pl.ds(b_base, DEEP), 0:16] = b_in[off : off + DEEP]
            X[c, pl.ds(b_base, DEEP), 16:24] = at.y_part(y2[N_SLOTS + off : N_SLOTS + off + DEEP])
    zs = 2 * N_SLOTS
    for f, X, S in ((PERM, I, SI), (SEED, PS.at[top], SP.at[top])):
        for c in range(3):
            q = 3 * f + c
            t = q // 4
            own = jnp.concatenate([z_in[t], at.y_part(yz[t])], axis=0)
            from_a = jnp.concatenate([za_in[t], at.y_part(y2[zs + t])], axis=0)
            from_b = jnp.concatenate([zb_in[t], at.y_part(y2[zs + 2 + t])], axis=0)
            above = jnp.where(at.even, from_a, from_b)
            below = jnp.where(at.even, from_b, from_a)
            halo = jnp.where(lane < 64, above, below)
            around = [X[c, DEEP + cx + k] for k in range(DEEP)] + [jnp.zeros((24, 128), F32)] * 2
            around += [X[c, k] for k in range(DEEP)]
            tiles = [at.strip_tile([X[c, DEEP + x] for x in range(cx)], own, q), at.strip_tile(around, halo, q)]
            S[c] = jnp.concatenate(tiles, axis=1)

    s_shape = (24, 256)
    s_keep = jnp.where((rows_of(s_shape) >= 20) & at.no_low_y, 0.0, 1.0)
    s_keep = jnp.where((lanes_of(s_shape) >= 192) & at.no_low_x, 0.0, s_keep)

    def sx_up(v):
        return pltpu.roll(v, 240, 1)

    def sx_down(v):
        return pltpu.roll(v, 16, 1)

    def keep_at(x):
        return at.keep_row * jnp.where(at.no_low_x, 0.0, 1.0) if x < DEEP else at.keep_row

    def sweep(lo, hi, body):
        for first in range(lo, hi, 8):
            body(list(range(first, min(first + 8, hi))))

    def halve(xs):
        new = []
        for x in xs:
            half = tuple(time_step * v for v in get(I, x))
            new.append((half, tuple(a * b for a, b in zip(half, get(PS.at[top], x)))))
        put(I, xs, [n[0] for n in new])
        put(W, xs, [n[1] for n in new])

    sweep(0, last, halve)
    for c in range(3):
        W[c, last] = jnp.zeros((24, 128), F32)
        i_out[c] = I[c, 1 : 1 + i_out.shape[1]]
    half = tuple(time_step * v for v in sget(SI))
    sput(SI, half)
    sput(si_out, half)
    sput(SW, tuple(a * b for a, b in zip(half, sget(SP.at[top]))))

    for m in range(STEPS - 1):
        n = top - m

        def magnetic(xs, m=m):
            new = []
            for x in xs:
                curl = curl_f(get(W, x), get(W, x + 1, (1, 2)), y_up, at.z_up)
                keep = keep_at(x)
                if m == 0:
                    new.append(tuple(keep * v for v in curl))
                else:
                    new.append(tuple(q + keep * v for q, v in zip(get(M, x), curl)))
            put(M, xs, new)

        def electric(xs, m=m, n=n):
            new = []
            for x in xs:
                curl = curl_b(get(M, x), get(M, x - 1, (1, 2)), y_down, at.z_down)
                p = tuple(q - time_step * v for q, v in zip(get(PS.at[n], x), curl))
                new.append((p, tuple(a * b for a, b in zip(get(I, x), p))))
            put(PS.at[n - 1], xs, [v[0] for v in new])
            if m < STEPS - 2:
                put(W, xs, [v[1] for v in new])

        sweep(m, last - 1 - m, magnetic)
        v = sget(SW)
        curl = curl_f(v, (sx_up(v[1]), sx_up(v[2])), y_up, sz_up)
        if m == 0:
            merged = tuple(s_keep * v for v in curl)
        else:
            merged = tuple(q + s_keep * v for q, v in zip(sget(SM), curl))
        sput(SM, merged)
        curl = curl_b(merged, (sx_down(merged[1]), sx_down(merged[2])), y_down, sz_down)
        p = tuple(q - time_step * v for q, v in zip(sget(SP.at[n]), curl))
        sput(SP.at[n - 1], p)
        sput(SW, tuple(a * b for a, b in zip(sget(SI), p)))
        sweep(m + 1, last - 1 - m, electric)

    for c in range(3):
        for x in range(cx):
            g = jnp.zeros((16, 128), F32)
            for n in range(STEPS):
                p = PS[n, c, DEEP + x, 0:16]
                g = g + p * c_own[n, c, x]
                if n < top:
                    p_out[n, c, x] = p
            g_out[c, x] = g
        g = jnp.zeros((24, 128), F32)
        for n in range(STEPS):
            p = SP[n, c, :, 0:128]
            g = g + p * sc_own[n, c]
            sp_out[n, c] = p
        sg_out[c] = g


LOW_H = ([-1], [-2, -1, 0], [-2, -1, 0, 1], [-1, 0, 1, 2])
LOW_E = ([-1, 0], [-2, -1, 0, 1], [-1, 0, 1, 2], [0, 1, 2, 3])
HIGH_H = ([-1], [-2, -1, 0], [-3, -2, -1, 0], [-4, -3, -2, -1])
HIGH_E = ([-1, 0], [-2, -1, 0, 1], [-3, -2, -1, 0], [-4, -3, -2, -1])


def driven_kernel(sd_in, a_sent, b_sent, a_in, b_in, e_own, se_own, i_in, si_in, p_in, sp_in, g_own, sg_own, ids,
                  e_out, s_out, E, H, G):
    at = Place()
    cx = e_own.shape[1]
    lane = at.lane
    base = 3
    zero = jnp.zeros((24, 128), F32)
    for c in range(3):
        for x in range(E.shape[1]):
            E[c, x] = zero
            H[c, x] = zero
        G[c] = g_own[c]

    def traces(a, b, i):
        return jnp.where(at.even, a[i], b[i])

    def upper(i):
        return traces(a_in, b_in, i)

    def lower(i):
        return traces(b_in, a_in, i)

    def own_up(i):
        return traces(a_sent, b_sent, i)

    def own_down(i):
        return traces(b_sent, a_sent, i)

    s_upper, s_lower, s_own_up, s_own_down = (t(N_TRACES) for t in (upper, lower, own_up, own_down))
    s_shape = (24, 256)
    s_keep = jnp.where((rows_of(s_shape) >= 20) & at.no_low_y, 0.0, time_step)
    s_keep = jnp.where((lanes_of(s_shape) >= 192) & at.no_low_x, 0.0, s_keep)

    def source(first, second, i, group):
        tiles = [pltpu.roll(v, (16 * (group - i)) % 128, 1) for v in (first, second)]
        return jnp.concatenate([jnp.where(lane // 16 == group, v, 0.0) for v in tiles], axis=1)

    si = sget(si_in)
    se = sh = (jnp.zeros(s_shape, F32),) * 3
    sg = sget(sg_own)
    for n in range(STEPS):
        xs = LOW_H[n] + [cx + x for x in HIGH_H[n]]
        new = []
        for x in xs:
            nxt = get(E, base + x + 1, (1, 2))
            if x == -1:
                nxt = tuple(v + own_down(2 * n + k) for k, v in enumerate(nxt))
            if x == cx - 1:
                nxt = tuple(v + upper(2 * n + k) for k, v in enumerate(nxt))
            curl = curl_f(get(E, base + x), nxt, y_up, at.z_up)
            keep = time_step * at.keep_row
            if x < 0:
                keep = keep * jnp.where(at.no_low_x, 0.0, 1.0)
            new.append(tuple(q - keep * v for q, v in zip(get(H, base + x), curl)))
        put(H, [base + x for x in xs], new)
        nxt = tuple(pltpu.roll(se[1 + k], 240, 1) + source(s_upper, s_own_down, 2 * n + k, 7) for k in range(2))
        curl = curl_f(se, nxt, y_up, sz_up)
        sh = tuple(q - s_keep * v for q, v in zip(sh, curl))

        xs = LOW_E[n] + [cx + x for x in HIGH_E[n]]
        new, grads = [], []
        for x in xs:
            prv = get(H, base + x - 1, (1, 2))
            if x == 0:
                prv = tuple(v + lower(2 * n + k) for k, v in enumerate(prv))
            if x == cx:
                prv = tuple(v + own_up(2 * n + k) for k, v in enumerate(prv))
            curl = curl_b(get(H, base + x), prv, y_down, at.z_down)
            new.append(tuple(q + i * v for q, i, v in zip(get(E, base + x), get(i_in, 2 + x), curl)))
            grads.append(curl)
        put(E, [base + x for x in xs], new)
        for x, curl in zip(xs, grads):
            if 0 <= x < cx:
                for c in range(3):
                    p = sd_in[c, x] if n == STEPS - 1 else p_in[n, c, x]
                    G[c, x] += p * curl[c][0:16]
        prv = tuple(pltpu.roll(sh[1 + k], 16, 1) + source(s_lower, s_own_up, 2 * n + k, 0) for k in range(2))
        curl = curl_b(sh, prv, y_down, sz_down)
        se = tuple(q + i * v for q, i, v in zip(se, si, curl))
        sg = tuple(g + sp_in[n, c] * curl[c][:, 0:128] for c, g in enumerate(sg))

    lane16 = lanes_of((16, 128))
    seam_lo = jnp.where(at.gz == 0, 128 - EDGE, 0)
    seam = (lane16 >= seam_lo) & (lane16 < seam_lo + EDGE)
    s_elec = [(se[c][0:16, 0:128] + se_own[c, 0:16]) for c in range(3)]
    s_grad = [sg[c][0:16] for c in range(3)]

    def with_seam(plane, strip, x):
        moved = pltpu.roll(strip, (seam_lo - 16 * x - EDGE + 256) % 128, 1)
        return jnp.where(seam, moved, plane)

    acc = jnp.zeros((80, 128), F32)
    for x in range(cx):
        grads = []
        for c in range(3):
            e_out[c, x] = with_seam(E[c, base + x, 0:16] + e_own[c, x], s_elec[c], x)
            grads.append(with_seam(G[c, x], s_grad[c], x))
        lhs, rhs = [], []
        for r in range(2):
            g = jnp.concatenate([v[8 * r : 8 * r + 8] for v in grads], axis=0)
            one = g.astype(jnp.bfloat16).astype(F32)
            rest = g - one
            two = rest.astype(jnp.bfloat16).astype(F32)
            three = rest - two
            lhs.append(jnp.concatenate([one, two, three, jnp.zeros((8, 128), F32)], axis=0).astype(jnp.bfloat16))
            region = ids[x, 8 * r : 8 * r + 8]
            slot = jnp.where(
                region < at.second_owner * REG_DEV,
                region - at.first_owner * REG_DEV,
                region - at.second_owner * REG_DEV + REG_DEV,
            )
            hot = jnp.concatenate([jnp.where(slot == s, 1.0, 0.0) for s in range(2 * REG_DEV)], axis=0)
            rhs.append(hot.astype(jnp.bfloat16))
        acc = acc + lax.dot_general(
            jnp.concatenate(lhs, axis=1),
            jnp.concatenate(rhs, axis=1),
            (((1,), (1,)), ((), ())),
            preferred_element_type=F32,
        )
    sums = acc[0:24] + acc[24:48] + acc[48:72]
    sums = jnp.where(rows_of((24, 128)) % 8 == lanes_of((24, 128)) % 8, sums, 0.0)
    parts = [jnp.sum(sums[8 * c : 8 * c + 8], axis=0, keepdims=True) for c in range(3)]
    parts = jnp.concatenate(parts + [jnp.zeros((5, 128), F32)], axis=0)
    fold = jnp.where(rows_of((128, 128)) // 8 == lanes_of((128, 128)), time_step * grad_scale, 0.0)
    s_out[...] = jnp.dot(parts, fold, precision=lax.Precision.HIGHEST, preferred_element_type=F32)


def y_rows(v):
    first = lax.broadcasted_iota(jnp.int32, (1, 8, 1), 1) < EDGE
    return jnp.where(first, v[:, 0:8], v[:, 8:16])


def local(e_start, h_start, inv_perm, adj_seed, region_ids):
    n_gx, n_gy = lax.axis_size("gx"), lax.axis_size("gy")
    xi = lax.axis_index("gx")
    cx = e_start.shape[1]
    even = (xi + 1) % 2
    vmem = pl.BlockSpec(memory_space=pltpu.VMEM)
    shape = lambda *dims: jax.ShapeDtypeStruct(dims, F32)
    tile = lambda *dims: pltpu.VMEM(dims, F32)

    a_pairs = [(i, i ^ 1) for i in range(n_gx)]
    b_pairs = [(i, ((i - 1) ^ 1) + 1) for i in range(1, n_gx - 1)]

    def swap_y(v):
        if n_gy == 2:
            return lax.ppermute(v, "gy", [(0, 1), (1, 0)])
        up = lax.ppermute(v, "gy", [(i, i + 1) for i in range(n_gy - 1)])
        down = lax.ppermute(v, "gy", [(i + 1, i) for i in range(n_gy - 1)])
        first = lax.broadcasted_iota(jnp.int32, (1, 8, 1), 1) < EDGE
        return jnp.where(first, down, up)

    def call(kernel, outs, scratch, args, mib, specs=None):
        return pl.pallas_call(
            kernel,
            out_shape=outs,
            in_specs=specs or [vmem] * len(args),
            out_specs=(vmem,) * len(outs),
            scratch_shapes=scratch,
            compiler_params=pltpu.CompilerParams(vmem_limit_bytes=mib * 1024 * 1024),
        )(*args)

    own = tile(*e_start.shape)
    a_msg, b_msg, z_msg, y_msg = call(
        pack_kernel,
        (shape(N_SLOTS, 16, 128), shape(N_SLOTS, 16, 128), shape(3, 16, 128), shape(12 * cx, 8, 128)),
        [own] * 4 + [pltpu.SemaphoreType.DMA((4,))],
        tuple(pltpu.with_memory_space_constraint(v, pltpu.HBM) for v in (inv_perm, adj_seed, e_start, h_start)),
        8,
        [pl.BlockSpec(memory_space=pltpu.HBM)] * 4,
    )
    z_got = lax.ppermute(z_msg, "gz", [(0, 1), (1, 0)])
    y1 = swap_y(y_msg)
    a_got = lax.ppermute(a_msg, "gx", a_pairs)
    b_got = lax.ppermute(b_msg, "gx", b_pairs)
    yz = swap_y(y_rows(z_got))
    za_got = lax.ppermute(z_got[0:2], "gx", a_pairs)
    zb_got = lax.ppermute(z_got[0:2], "gx", b_pairs)

    n_msg = N_TRACES + 1
    field = tile(3, cx + 2, 24, 128)
    a_sent, b_sent, c_own, e_own, sc_own, se_own = call(
        own_kernel,
        (
            shape(n_msg, 24, 128),
            shape(n_msg, 24, 128),
            shape(STEPS, 3, cx, 16, 128),
            shape(3, cx, 16, 128),
            shape(STEPS, 3, 24, 128),
            shape(3, 24, 128),
        ),
        [field] * 3,
        (inv_perm, e_start, h_start, y1, z_got, yz),
        8,
    )
    a_in = lax.ppermute(a_sent, "gx", a_pairs)
    b_in = lax.ppermute(b_sent, "gx", b_pairs)
    a_got, b_got, za_got, zb_got, _ = lax.optimization_barrier((a_got, b_got, za_got, zb_got, a_sent))
    y2 = swap_y(jnp.concatenate([y_rows(v) for v in (a_got, b_got, za_got, zb_got)], axis=0))

    planes = cx + 2 * DEEP + 1
    field = tile(3, planes, 24, 128)
    strip = tile(3, 24, 256)
    i_ext, si_ext, p_own, sp_own, g_own, sg_own = call(
        adjoint_kernel,
        (
            shape(3, cx + 4, 24, 128),
            shape(3, 24, 256),
            shape(STEPS - 1, 3, cx, 16, 128),
            shape(STEPS, 3, 24, 128),
            shape(3, cx, 16, 128),
            shape(3, 24, 128),
        ),
        [field] * 3 + [tile(STEPS, 3, planes, 24, 128)] + [strip] * 3 + [tile(STEPS, 3, 24, 256)],
        (inv_perm, adj_seed, a_got, b_got, z_got, za_got, zb_got, y1, yz, y2, c_own, sc_own),
        12,
    )
    field = tile(3, cx + 5, 24, 128)
    e_field, sums = call(
        driven_kernel,
        (shape(*e_start.shape), shape(8, 128)),
        [field] * 2 + [own],
        (adj_seed, a_sent, b_sent, a_in, b_in, e_own, se_own, i_ext, si_ext, p_own, sp_own, g_own, sg_own, region_ids),
        8,
    )
    total = sums + lax.ppermute(sums, "gx", a_pairs)
    owned = jnp.where(even == 1, total[0:3, 0:REG_DEV], total[0:3, REG_DEV : 2 * REG_DEV])
    return e_field, owned


def solution(mesh):
    placed = (
        P(None, "gx", "gy", "gz"),
        P(None, "gx", "gy", "gz"),
        P(None, "gx", "gy", "gz"),
        P(None, "gx", "gy", "gz"),
        P("gx", "gy", "gz"),
    )
    return jax.shard_map(
        local,
        mesh=mesh,
        in_specs=placed,
        out_specs=(P(None, "gx", "gy", "gz"), P(None, ("gx", "gy", "gz"))),
        check_vma=False,
    )
```

```python
import jax
import jax.numpy as jnp
from jax import lax
from jax.experimental import pallas as pl
from jax.experimental.pallas import tpu as pltpu
from jax.sharding import PartitionSpec as P

STEPS = 4
REG_DEV = 8
DEEP = 3
EDGE = 4
PERM, SEED, ELEC, MAGN = range(4)
N_SLOTS = 2 * 3 * DEEP
N_TRACES = 2 * STEPS

time_step = 0.5
grad_scale = 1.0 / 64.0
F32 = jnp.float32


def lanes_of(shape):
    return lax.broadcasted_iota(jnp.int32, shape, len(shape) - 1)


def rows_of(shape):
    return lax.broadcasted_iota(jnp.int32, shape, len(shape) - 2)


def roll_up(v, axis):
    return pltpu.roll(v, v.shape[axis] - 1, axis)


def roll_down(v, axis):
    return pltpu.roll(v, 1, axis)


def curl_f(v, nxt, shift_y, shift_z):
    vx, vy, vz = v
    ny, nz = nxt
    return (
        (shift_y(vz) - vz) - (shift_z(vy) - vy),
        (shift_z(vx) - vx) - (nz - vz),
        (ny - vy) - (shift_y(vx) - vx),
    )


def curl_b(v, prv, shift_y, shift_z):
    vx, vy, vz = v
    py, pz = prv
    return (
        (vz - shift_y(vz)) - (vy - shift_z(vy)),
        (vx - shift_z(vx)) - (vz - pz),
        (vy - py) - (vx - shift_y(vx)),
    )


class Place:
    def __init__(self):
        xi, yi, self.gz = (lax.axis_index(a) for a in ("gx", "gy", "gz"))
        n_gy, n_gz = lax.axis_size("gy"), lax.axis_size("gz")
        even = (xi + 1) % 2
        self.even = even == 1
        self.no_low_x = xi == 0
        self.no_low_y = yi == 0
        self.no_high_y = yi == n_gy - 1
        own_flat = xi * n_gy * n_gz + yi * n_gz + self.gz
        self.first_owner = own_flat - (1 - even) * n_gy * n_gz
        self.second_owner = self.first_owner + n_gy * n_gz
        self.lane = lanes_of((24, 128))
        self.row = rows_of((24, 128))
        self.keep_row = jnp.where((self.row >= 20) & self.no_low_y, 0.0, 1.0)
        self.own_off = jnp.where(self.gz == 0, 8, 4)
        self.own_j = jnp.where(self.gz == 0, 0, 4)
        self.got_j = jnp.where(self.gz == 0, 8, 0)

    def y_part(self, v):
        high = jnp.where(self.no_high_y, 0.0, 1.0)
        low = jnp.where(self.no_low_y, 0.0, 1.0)
        return v * jnp.where(rows_of(v.shape[-2:]) < EDGE, high, low)

    def strip_own(self, planes):
        lane = self.lane
        acc = jnp.zeros((24, 128), F32)
        for x, plane in enumerate(planes):
            acc = jnp.where(lane // 16 == x, pltpu.roll(plane, (16 * x + self.own_off) % 128, 1), acc)
        j = lane % 16
        return jnp.where((j >= self.own_j) & (j < self.own_j + 8), acc, 0.0)

    def strip_got(self, tile, got, q):
        j = self.lane % 16
        got = pltpu.roll(got, (self.got_j - 4 * (q % 4) + 128) % 128, 1)
        return jnp.where((j >= self.got_j) & (j < self.got_j + EDGE), got, tile)

    def z_up(self, v):
        return jnp.where(self.lane == 127, 0.0, roll_up(v, 1))

    def z_down(self, v):
        return jnp.where(self.lane == 0, 0.0, roll_down(v, 1))


def y_up(v):
    return roll_up(v, 0)


def y_down(v):
    return roll_down(v, 0)


def sz_up(v):
    return roll_up(v, 1)


def sz_down(v):
    return roll_down(v, 1)


def get(ref, x, comps=(0, 1, 2)):
    return tuple(ref[c, x] for c in comps)


def put(ref, xs, values):
    for x, v in zip(xs, values):
        for c in range(3):
            ref[c, x] = v[c]


def sget(ref):
    return tuple(ref[c] for c in range(3))


def sput(ref, v):
    for c in range(3):
        ref[c] = v[c]


def pack_kernel(ip_hbm, sd_hbm, e_hbm, h_hbm, a_out, b_out, z_out, y_out, ip, sd, e, h, sems):
    even, gz = (lax.axis_index("gx") + 1) % 2, lax.axis_index("gz")
    refs = (ip, sd, e, h)
    copies = []
    for i, src in enumerate((ip_hbm, sd_hbm, e_hbm, h_hbm)):
        copies.append(pltpu.make_async_copy(src, refs[i], sems.at[i]))
    for copy in copies:
        copy.start()
    for copy in copies:
        copy.wait()
    cx = e.shape[1]
    a_base = jnp.where(even == 1, cx - DEEP, 0)
    b_base = jnp.where(even == 1, 0, cx - DEEP)
    for f in (PERM, SEED):
        for c in range(3):
            off = DEEP * (3 * f + c)
            a_out[off : off + DEEP] = refs[f][c, pl.ds(a_base, DEEP)]
            b_out[off : off + DEEP] = refs[f][c, pl.ds(b_base, DEEP)]
    group = lanes_of((16, 128)) // EDGE
    z_off = jnp.where(gz == 0, EDGE, 0)
    for t in range(3):
        total = jnp.zeros((16, 128), F32)
        for k in range(4):
            f, c = divmod(4 * t + k, 3)
            for x in range(cx):
                moved = pltpu.roll(refs[f][c, x], (16 * x + 4 * k + z_off) % 128, 1)
                total = jnp.where(group == 4 * x + k, moved, total)
        z_out[t] = total
    first = rows_of((cx, 8, 128)) < EDGE
    for f in range(4):
        for c in range(3):
            q = 3 * f + c
            y_out[q * cx : (q + 1) * cx] = jnp.where(first, refs[f][c, :, 0:8], refs[f][c, :, 8:16])


def own_kernel(ip_in, e_in, h_in, y1, z_in, yz,
               a_out, b_out, c_out, e_out, sc_out, se_out, I, E, H):
    at = Place()
    cx = e_in.shape[1]
    lane = at.lane
    zero = jnp.zeros((24, 128), F32)
    strips = []
    for f, X, src in ((PERM, I, ip_in), (ELEC, E, e_in), (MAGN, H, h_in)):
        strip = []
        for c in range(3):
            q = 3 * f + c
            X[c, 0] = zero
            X[c, cx + 1] = zero
            X[c, 1 : cx + 1, 0:16] = src[c]
            X[c, 1 : cx + 1, 16:24] = at.y_part(y1[q * cx : (q + 1) * cx])
            if f == PERM:
                X[c] = time_step * X[c]
            got = jnp.concatenate([z_in[q // 4], at.y_part(yz[q // 4])], axis=0)
            tile = at.strip_own([X[c, x] for x in range(1, cx + 1)])
            tile = at.strip_got(tile, time_step * got if f == PERM else got, q)
            strip.append(tile)
        strips.append(tuple(strip))
    si, se, sh = strips

    def sx_up(v):
        return jnp.where(lane >= 112, 0.0, pltpu.roll(v, 112, 1))

    def sx_down(v):
        return jnp.where(lane < 16, 0.0, pltpu.roll(v, 16, 1))

    xs = list(range(1, cx + 1))
    up_strip, down_strip = zero, zero
    for n in range(STEPS):
        downs = get(E, 1, (1, 2))
        new = []
        for x in xs:
            curl = curl_f(get(E, x), get(E, x + 1, (1, 2)), y_up, at.z_up)
            keep = time_step * at.keep_row
            new.append(tuple(q - keep * v for q, v in zip(get(H, x), curl)))
        put(H, xs, new)
        curl = curl_f(se, (sx_up(se[1]), sx_up(se[2])), y_up, sz_up)
        down_from = se
        sh = tuple(q - time_step * at.keep_row * v for q, v in zip(sh, curl))
        ups = get(H, cx, (1, 2))
        new, curls = [], []
        for x in xs:
            curl = curl_b(get(H, x), get(H, x - 1, (1, 2)), y_down, at.z_down)
            new.append(tuple(q + i * v for q, i, v in zip(get(E, x), get(I, x), curl)))
            curls.append(curl)
        put(E, xs, new)
        for x, curl in zip(xs, curls):
            for c in range(3):
                c_out[n, c, x - 1] = curl[c][0:16]
        curl = curl_b(sh, (sx_down(sh[1]), sx_down(sh[2])), y_down, sz_down)
        se = tuple(q + i * v for q, i, v in zip(se, si, curl))
        for c in range(3):
            sc_out[n, c] = curl[c]
        for k in range(2):
            i = 2 * n + k
            a_out[i] = jnp.where(at.even, ups[k], downs[k])
            b_out[i] = jnp.where(at.even, downs[k], ups[k])
            here = lane // 16 == i
            up_strip = jnp.where(here, pltpu.roll(sh[1 + k], (16 * i + 16) % 128, 1), up_strip)
            down_strip = jnp.where(here, pltpu.roll(down_from[1 + k], 16 * i, 1), down_strip)
    edges = [jnp.concatenate([z_in[t], at.y_part(yz[t])], axis=0) for t in range(2)]
    up_edges = jnp.where(lane < 64, pltpu.roll(edges[0], 64, 1), edges[1])
    down_edges = jnp.where(lane < 64, edges[0], pltpu.roll(edges[1], 64, 1))
    a_out[N_TRACES + 1] = jnp.where(at.even, up_edges, down_edges)
    b_out[N_TRACES + 1] = jnp.where(at.even, down_edges, up_edges)
    a_out[N_TRACES] = jnp.where(at.even, up_strip, down_strip)
    b_out[N_TRACES] = jnp.where(at.even, down_strip, up_strip)
    for c in range(3):
        e_out[c] = E[c, 1 : cx + 1, 0:16]
    sput(se_out, se)


def adjoint_kernel(ip_in, sd_in, a_in, b_in, z_in, y1, yz, y2, c_own,
                   i_out, s_out, p_out, g_out, I, W, M, PS):
    at = Place()
    cx = ip_in.shape[1]
    lane = at.lane
    last = cx + 2 * DEEP
    top = STEPS - 1
    a_base = jnp.where(at.even, DEEP + cx, 0)
    b_base = jnp.where(at.even, 0, DEEP + cx)
    for f, X, src in ((PERM, I, ip_in), (SEED, PS.at[top], sd_in)):
        for c in range(3):
            q = 3 * f + c
            off = DEEP * q
            X[c, last] = jnp.zeros((24, 128), F32)
            X[c, DEEP : DEEP + cx, 0:16] = src[c]
            X[c, DEEP : DEEP + cx, 16:24] = at.y_part(y1[q * cx : (q + 1) * cx])
            X[c, pl.ds(a_base, DEEP), 0:16] = a_in[off : off + DEEP]
            X[c, pl.ds(a_base, DEEP), 16:24] = at.y_part(y2[off : off + DEEP])
            X[c, pl.ds(b_base, DEEP), 0:16] = b_in[off : off + DEEP]
            X[c, pl.ds(b_base, DEEP), 16:24] = at.y_part(y2[N_SLOTS + off : N_SLOTS + off + DEEP])
    for f, X in ((PERM, I), (SEED, PS.at[top])):
        for c in range(3):
            q = 3 * f + c
            t = q // 4
            own = jnp.concatenate([z_in[t], at.y_part(yz[t])], axis=0)
            around = [X[c, DEEP + cx + k] for k in range(DEEP)] + [jnp.zeros((24, 128), F32)] * 2
            around += [X[c, k] for k in range(DEEP)]
            s_out[q, :, 0:128] = at.strip_got(at.strip_own([X[c, DEEP + x] for x in range(cx)]), own, q)
            s_out[q, :, 128:256] = at.strip_own(around)

    def keep_at(x):
        return at.keep_row * jnp.where(at.no_low_x, 0.0, 1.0) if x < DEEP else at.keep_row

    def sweep(lo, hi, body):
        for first in range(lo, hi, 8):
            body(list(range(first, min(first + 8, hi))))

    def halve(xs):
        new = []
        for x in xs:
            half = tuple(time_step * v for v in get(I, x))
            new.append((half, tuple(a * b for a, b in zip(half, get(PS.at[top], x)))))
        put(I, xs, [n[0] for n in new])
        put(W, xs, [n[1] for n in new])

    sweep(0, last, halve)
    for c in range(3):
        W[c, last] = jnp.zeros((24, 128), F32)
        i_out[c] = I[c, 1 : 1 + i_out.shape[1]]

    for m in range(STEPS - 1):
        n = top - m

        def magnetic(xs, m=m):
            new = []
            for x in xs:
                curl = curl_f(get(W, x), get(W, x + 1, (1, 2)), y_up, at.z_up)
                keep = keep_at(x)
                if m == 0:
                    new.append(tuple(keep * v for v in curl))
                else:
                    new.append(tuple(q + keep * v for q, v in zip(get(M, x), curl)))
            put(M, xs, new)

        def electric(xs, m=m, n=n):
            new = []
            for x in xs:
                curl = curl_b(get(M, x), get(M, x - 1, (1, 2)), y_down, at.z_down)
                p = tuple(q - time_step * v for q, v in zip(get(PS.at[n], x), curl))
                new.append((p, tuple(a * b for a, b in zip(get(I, x), p))))
            put(PS.at[n - 1], xs, [v[0] for v in new])
            if m < STEPS - 2:
                put(W, xs, [v[1] for v in new])

        sweep(m, last - 1 - m, magnetic)
        sweep(m + 1, last - 1 - m, electric)

    for c in range(3):
        for x in range(cx):
            g = jnp.zeros((16, 128), F32)
            for n in range(STEPS):
                p = PS[n, c, DEEP + x, 0:16]
                g = g + p * c_own[n, c, x]
                if n < top:
                    p_out[n, c, x] = p
            g_out[c, x] = g


LOW_H = ([-1], [-2, -1, 0], [-2, -1, 0, 1], [-1, 0, 1, 2])
LOW_E = ([-1, 0], [-2, -1, 0, 1], [-1, 0, 1, 2], [0, 1, 2, 3])
HIGH_H = ([-1], [-2, -1, 0], [-3, -2, -1, 0], [-4, -3, -2, -1])
HIGH_E = ([-1, 0], [-2, -1, 0, 1], [-3, -2, -1, 0], [-4, -3, -2, -1])


def driven_kernel(sd_in, a_sent, b_sent, a_in, b_in, e_own, sc_own, se_own, i_in, s_in, p_in, g_own, ids,
                  e_out, s_out, E, H, G):
    at = Place()
    cx = e_own.shape[1]
    lane = at.lane
    base = 3
    zero = jnp.zeros((24, 128), F32)
    for c in range(3):
        for x in range(E.shape[1]):
            E[c, x] = zero
            H[c, x] = zero
        G[c] = g_own[c]

    def traces(a, b, i):
        return jnp.where(at.even, a[i], b[i])

    def upper(i):
        return traces(a_in, b_in, i)

    def lower(i):
        return traces(b_in, a_in, i)

    def own_up(i):
        return traces(a_sent, b_sent, i)

    def own_down(i):
        return traces(b_sent, a_sent, i)

    s_upper, s_lower, s_own_up, s_own_down = (t(N_TRACES) for t in (upper, lower, own_up, own_down))
    s_shape = (24, 256)
    s_keep = jnp.where((rows_of(s_shape) >= 20) & at.no_low_y, 0.0, time_step)
    s_keep = jnp.where((lanes_of(s_shape) >= 192) & at.no_low_x, 0.0, s_keep)

    def source(first, second, i, group):
        tiles = [pltpu.roll(v, (16 * (group - i)) % 128, 1) for v in (first, second)]
        return jnp.concatenate([jnp.where(lane // 16 == group, v, 0.0) for v in tiles], axis=1)

    above, below = upper(N_TRACES + 1), lower(N_TRACES + 1)
    edges = (
        jnp.where(lane < 64, above, pltpu.roll(below, 64, 1)),
        jnp.where(lane < 64, pltpu.roll(above, 64, 1), below),
    )
    strips = []
    for q in range(6):
        tile = at.strip_got(s_in[q, :, 128:256], edges[q // 4], q)
        strips.append(jnp.concatenate([s_in[q, :, 0:128], tile], axis=1))
    si = tuple(time_step * v for v in strips[0:3])
    sp = tuple(strips[3:6])
    adjoint = [None] * (STEPS - 1) + [sp]
    sm = (0.0, 0.0, 0.0)
    for n in range(STEPS - 1, 0, -1):
        sw = tuple(a * b for a, b in zip(si, sp))
        curl = curl_f(sw, [pltpu.roll(v, 240, 1) for v in sw[1:]], y_up, sz_up)
        sm = tuple(q + 2.0 * s_keep * v for q, v in zip(sm, curl))
        curl = curl_b(sm, [pltpu.roll(v, 16, 1) for v in sm[1:]], y_down, sz_down)
        sp = tuple(q - time_step * v for q, v in zip(sp, curl))
        adjoint[n - 1] = sp

    se = sh = (jnp.zeros(s_shape, F32),) * 3
    sg = (0.0, 0.0, 0.0)
    for n in range(STEPS):
        xs = LOW_H[n] + [cx + x for x in HIGH_H[n]]
        new = []
        for x in xs:
            nxt = get(E, base + x + 1, (1, 2))
            if x == -1:
                nxt = tuple(v + own_down(2 * n + k) for k, v in enumerate(nxt))
            if x == cx - 1:
                nxt = tuple(v + upper(2 * n + k) for k, v in enumerate(nxt))
            curl = curl_f(get(E, base + x), nxt, y_up, at.z_up)
            keep = time_step * at.keep_row
            if x < 0:
                keep = keep * jnp.where(at.no_low_x, 0.0, 1.0)
            new.append(tuple(q - keep * v for q, v in zip(get(H, base + x), curl)))
        put(H, [base + x for x in xs], new)
        nxt = tuple(pltpu.roll(se[1 + k], 240, 1) + source(s_upper, s_own_down, 2 * n + k, 7) for k in range(2))
        curl = curl_f(se, nxt, y_up, sz_up)
        sh = tuple(q - s_keep * v for q, v in zip(sh, curl))

        xs = LOW_E[n] + [cx + x for x in HIGH_E[n]]
        new, grads = [], []
        for x in xs:
            prv = get(H, base + x - 1, (1, 2))
            if x == 0:
                prv = tuple(v + lower(2 * n + k) for k, v in enumerate(prv))
            if x == cx:
                prv = tuple(v + own_up(2 * n + k) for k, v in enumerate(prv))
            curl = curl_b(get(H, base + x), prv, y_down, at.z_down)
            new.append(tuple(q + i * v for q, i, v in zip(get(E, base + x), get(i_in, 2 + x), curl)))
            grads.append(curl)
        put(E, [base + x for x in xs], new)
        for x, curl in zip(xs, grads):
            if 0 <= x < cx:
                for c in range(3):
                    p = sd_in[c, x] if n == STEPS - 1 else p_in[n, c, x]
                    G[c, x] += p * curl[c][0:16]
        prv = tuple(pltpu.roll(sh[1 + k], 16, 1) + source(s_lower, s_own_up, 2 * n + k, 0) for k in range(2))
        curl = curl_b(sh, prv, y_down, sz_down)
        se = tuple(q + i * v for q, i, v in zip(se, si, curl))
        sg = tuple(
            g + adjoint[n][c][:, 0:128] * (curl[c][:, 0:128] + sc_own[n, c]) for c, g in enumerate(sg)
        )

    lane16 = lanes_of((16, 128))
    seam_lo = jnp.where(at.gz == 0, 128 - EDGE, 0)
    seam = (lane16 >= seam_lo) & (lane16 < seam_lo + EDGE)
    s_elec = [(se[c][0:16, 0:128] + se_own[c, 0:16]) for c in range(3)]
    s_grad = [sg[c][0:16] for c in range(3)]

    def with_seam(plane, strip, x):
        moved = pltpu.roll(strip, (seam_lo - 16 * x - EDGE + 256) % 128, 1)
        return jnp.where(seam, moved, plane)

    acc = jnp.zeros((80, 128), F32)
    for x in range(cx):
        grads = []
        for c in range(3):
            e_out[c, x] = with_seam(E[c, base + x, 0:16] + e_own[c, x], s_elec[c], x)
            grads.append(with_seam(G[c, x], s_grad[c], x))
        lhs, rhs = [], []
        for r in range(2):
            g = jnp.concatenate([v[8 * r : 8 * r + 8] for v in grads], axis=0)
            one = g.astype(jnp.bfloat16).astype(F32)
            rest = g - one
            two = rest.astype(jnp.bfloat16).astype(F32)
            three = rest - two
            lhs.append(jnp.concatenate([one, two, three, jnp.zeros((8, 128), F32)], axis=0).astype(jnp.bfloat16))
            region = ids[x, 8 * r : 8 * r + 8]
            slot = jnp.where(
                region < at.second_owner * REG_DEV,
                region - at.first_owner * REG_DEV,
                region - at.second_owner * REG_DEV + REG_DEV,
            )
            hot = jnp.concatenate([jnp.where(slot == s, 1.0, 0.0) for s in range(2 * REG_DEV)], axis=0)
            rhs.append(hot.astype(jnp.bfloat16))
        acc = acc + lax.dot_general(
            jnp.concatenate(lhs, axis=1),
            jnp.concatenate(rhs, axis=1),
            (((1,), (1,)), ((), ())),
            preferred_element_type=F32,
        )
    sums = acc[0:24] + acc[24:48] + acc[48:72]
    sums = jnp.where(rows_of((24, 128)) % 8 == lanes_of((24, 128)) % 8, sums, 0.0)
    parts = [jnp.sum(sums[8 * c : 8 * c + 8], axis=0, keepdims=True) for c in range(3)]
    parts = jnp.concatenate(parts + [jnp.zeros((5, 128), F32)], axis=0)
    fold = jnp.where(rows_of((128, 128)) // 8 == lanes_of((128, 128)), time_step * grad_scale, 0.0)
    s_out[...] = jnp.dot(parts, fold, precision=lax.Precision.HIGHEST, preferred_element_type=F32)


def y_rows(v):
    first = lax.broadcasted_iota(jnp.int32, (1, 8, 1), 1) < EDGE
    return jnp.where(first, v[:, 0:8], v[:, 8:16])


def local(e_start, h_start, inv_perm, adj_seed, region_ids):
    n_gx, n_gy = lax.axis_size("gx"), lax.axis_size("gy")
    xi = lax.axis_index("gx")
    cx = e_start.shape[1]
    even = (xi + 1) % 2
    vmem = pl.BlockSpec(memory_space=pltpu.VMEM)
    shape = lambda *dims: jax.ShapeDtypeStruct(dims, F32)
    tile = lambda *dims: pltpu.VMEM(dims, F32)

    a_pairs = [(i, i ^ 1) for i in range(n_gx)]
    b_pairs = [(i, ((i - 1) ^ 1) + 1) for i in range(1, n_gx - 1)]

    def swap_y(v):
        if n_gy == 2:
            return lax.ppermute(v, "gy", [(0, 1), (1, 0)])
        up = lax.ppermute(v, "gy", [(i, i + 1) for i in range(n_gy - 1)])
        down = lax.ppermute(v, "gy", [(i + 1, i) for i in range(n_gy - 1)])
        first = lax.broadcasted_iota(jnp.int32, (1, 8, 1), 1) < EDGE
        return jnp.where(first, down, up)

    def call(kernel, outs, scratch, args, mib, specs=None):
        return pl.pallas_call(
            kernel,
            out_shape=outs,
            in_specs=specs or [vmem] * len(args),
            out_specs=(vmem,) * len(outs),
            scratch_shapes=scratch,
            compiler_params=pltpu.CompilerParams(vmem_limit_bytes=mib * 1024 * 1024),
        )(*args)

    own = tile(*e_start.shape)
    a_msg, b_msg, z_msg, y_msg = call(
        pack_kernel,
        (shape(N_SLOTS, 16, 128), shape(N_SLOTS, 16, 128), shape(3, 16, 128), shape(12 * cx, 8, 128)),
        [own] * 4 + [pltpu.SemaphoreType.DMA((4,))],
        tuple(pltpu.with_memory_space_constraint(v, pltpu.HBM) for v in (inv_perm, adj_seed, e_start, h_start)),
        8,
        [pl.BlockSpec(memory_space=pltpu.HBM)] * 4,
    )
    z_got = lax.ppermute(z_msg, "gz", [(0, 1), (1, 0)])
    y1 = swap_y(y_msg)
    a_got = lax.ppermute(a_msg, "gx", a_pairs)
    b_got = lax.ppermute(b_msg, "gx", b_pairs)
    yz = swap_y(y_rows(z_got))

    n_msg = N_TRACES + 2
    field = tile(3, cx + 2, 24, 128)
    a_sent, b_sent, c_own, e_own, sc_own, se_own = call(
        own_kernel,
        (
            shape(n_msg, 24, 128),
            shape(n_msg, 24, 128),
            shape(STEPS, 3, cx, 16, 128),
            shape(3, cx, 16, 128),
            shape(STEPS, 3, 24, 128),
            shape(3, 24, 128),
        ),
        [field] * 3,
        (inv_perm, e_start, h_start, y1, z_got, yz),
        8,
    )
    a_in = lax.ppermute(a_sent, "gx", a_pairs)
    b_in = lax.ppermute(b_sent, "gx", b_pairs)
    a_got, b_got, _ = lax.optimization_barrier((a_got, b_got, a_sent))
    y2 = swap_y(jnp.concatenate([y_rows(v) for v in (a_got, b_got)], axis=0))

    planes = cx + 2 * DEEP + 1
    field = tile(3, planes, 24, 128)
    i_ext, s_ext, p_own, g_own = call(
        adjoint_kernel,
        (
            shape(3, cx + 4, 24, 128),
            shape(6, 24, 256),
            shape(STEPS - 1, 3, cx, 16, 128),
            shape(3, cx, 16, 128),
        ),
        [field] * 3 + [tile(STEPS, 3, planes, 24, 128)],
        (inv_perm, adj_seed, a_got, b_got, z_got, y1, yz, y2, c_own),
        12,
    )
    field = tile(3, cx + 5, 24, 128)
    e_field, sums = call(
        driven_kernel,
        (shape(*e_start.shape), shape(8, 128)),
        [field] * 2 + [own],
        (adj_seed, a_sent, b_sent, a_in, b_in, e_own, sc_own, se_own, i_ext, s_ext, p_own, g_own, region_ids),
        8,
    )
    total = sums + lax.ppermute(sums, "gx", a_pairs)
    owned = jnp.where(even == 1, total[0:3, 0:REG_DEV], total[0:3, REG_DEV : 2 * REG_DEV])
    return e_field, owned


def solution(mesh):
    placed = (
        P(None, "gx", "gy", "gz"),
        P(None, "gx", "gy", "gz"),
        P(None, "gx", "gy", "gz"),
        P(None, "gx", "gy", "gz"),
        P("gx", "gy", "gz"),
    )
    return jax.shard_map(
        local,
        mesh=mesh,
        in_specs=placed,
        out_specs=(P(None, "gx", "gy", "gz"), P(None, ("gx", "gy", "gz"))),
        check_vma=False,
    )
```

```python
import jax
import jax.numpy as jnp
from jax import lax
from jax.experimental import pallas as pl
from jax.experimental.pallas import tpu as pltpu
from jax.sharding import PartitionSpec as P

STEPS = 4
REG_DEV = 8
DEEP = 3
EDGE = 4
PERM, SEED, ELEC, MAGN = range(4)
N_SLOTS = 2 * 3 * DEEP
N_TRACES = 2 * STEPS

time_step = 0.5
grad_scale = 1.0 / 64.0
F32 = jnp.float32


def lanes_of(shape):
    return lax.broadcasted_iota(jnp.int32, shape, len(shape) - 1)


def rows_of(shape):
    return lax.broadcasted_iota(jnp.int32, shape, len(shape) - 2)


def roll_up(v, axis):
    return pltpu.roll(v, v.shape[axis] - 1, axis)


def roll_down(v, axis):
    return pltpu.roll(v, 1, axis)


def curl_f(v, nxt, shift_y, shift_z):
    vx, vy, vz = v
    ny, nz = nxt
    return (
        (shift_y(vz) - vz) - (shift_z(vy) - vy),
        (shift_z(vx) - vx) - (nz - vz),
        (ny - vy) - (shift_y(vx) - vx),
    )


def curl_b(v, prv, shift_y, shift_z):
    vx, vy, vz = v
    py, pz = prv
    return (
        (vz - shift_y(vz)) - (vy - shift_z(vy)),
        (vx - shift_z(vx)) - (vz - pz),
        (vy - py) - (vx - shift_y(vx)),
    )


class Place:
    def __init__(self):
        xi, yi, self.gz = (lax.axis_index(a) for a in ("gx", "gy", "gz"))
        n_gy, n_gz = lax.axis_size("gy"), lax.axis_size("gz")
        even = (xi + 1) % 2
        self.even = even == 1
        self.no_low_x = xi == 0
        self.no_low_y = yi == 0
        self.no_high_y = yi == n_gy - 1
        own_flat = xi * n_gy * n_gz + yi * n_gz + self.gz
        self.first_owner = own_flat - (1 - even) * n_gy * n_gz
        self.second_owner = self.first_owner + n_gy * n_gz
        self.lane = lanes_of((24, 128))
        self.row = rows_of((24, 128))
        self.keep_row = jnp.where((self.row >= 20) & self.no_low_y, 0.0, 1.0)
        self.own_off = jnp.where(self.gz == 0, 8, 4)
        self.own_j = jnp.where(self.gz == 0, 0, 4)
        self.got_j = jnp.where(self.gz == 0, 8, 0)

    def y_part(self, v):
        high = jnp.where(self.no_high_y, 0.0, 1.0)
        low = jnp.where(self.no_low_y, 0.0, 1.0)
        return v * jnp.where(rows_of(v.shape[-2:]) < EDGE, high, low)

    def strip_own(self, planes):
        lane = self.lane
        acc = jnp.zeros((24, 128), F32)
        for x, plane in enumerate(planes):
            acc = jnp.where(lane // 16 == x, pltpu.roll(plane, (16 * x + self.own_off) % 128, 1), acc)
        j = lane % 16
        return jnp.where((j >= self.own_j) & (j < self.own_j + 8), acc, 0.0)

    def strip_got(self, tile, got, q):
        j = self.lane % 16
        got = pltpu.roll(got, (self.got_j - 4 * (q % 4) + 128) % 128, 1)
        return jnp.where((j >= self.got_j) & (j < self.got_j + EDGE), got, tile)

    def with_seam(self, plane, strip, x):
        lane = lanes_of((16, 128))
        lo = jnp.where(self.gz == 0, 128 - EDGE, 0)
        moved = pltpu.roll(strip, (lo - 16 * x - EDGE + 256) % 128, 1)
        return jnp.where((lane >= lo) & (lane < lo + EDGE), moved, plane)

    def z_up(self, v):
        return jnp.where(self.lane == 127, 0.0, roll_up(v, 1))

    def z_down(self, v):
        return jnp.where(self.lane == 0, 0.0, roll_down(v, 1))


def y_up(v):
    return roll_up(v, 0)


def y_down(v):
    return roll_down(v, 0)


def sz_up(v):
    return roll_up(v, 1)


def sz_down(v):
    return roll_down(v, 1)


def get(ref, x, comps=(0, 1, 2)):
    return tuple(ref[c, x] for c in comps)


def put(ref, xs, values):
    for x, v in zip(xs, values):
        for c in range(3):
            ref[c, x] = v[c]


def sget(ref):
    return tuple(ref[c] for c in range(3))


def sput(ref, v):
    for c in range(3):
        ref[c] = v[c]


def pack_kernel(ip_hbm, sd_hbm, e_hbm, h_hbm, a_out, b_out, z_out, y_out, ip, sd, e, h, sems):
    even, gz = (lax.axis_index("gx") + 1) % 2, lax.axis_index("gz")
    refs = (ip, sd, e, h)
    copies = []
    for i, src in enumerate((ip_hbm, sd_hbm, e_hbm, h_hbm)):
        copies.append(pltpu.make_async_copy(src, refs[i], sems.at[i]))
    for copy in copies:
        copy.start()
    for copy in copies:
        copy.wait()
    cx = e.shape[1]
    a_base = jnp.where(even == 1, cx - DEEP, 0)
    b_base = jnp.where(even == 1, 0, cx - DEEP)
    for f in (PERM, SEED):
        for c in range(3):
            off = DEEP * (3 * f + c)
            a_out[off : off + DEEP] = refs[f][c, pl.ds(a_base, DEEP)]
            b_out[off : off + DEEP] = refs[f][c, pl.ds(b_base, DEEP)]
    group = lanes_of((16, 128)) // EDGE
    z_off = jnp.where(gz == 0, EDGE, 0)
    for t in range(3):
        total = jnp.zeros((16, 128), F32)
        for k in range(4):
            f, c = divmod(4 * t + k, 3)
            for x in range(cx):
                moved = pltpu.roll(refs[f][c, x], (16 * x + 4 * k + z_off) % 128, 1)
                total = jnp.where(group == 4 * x + k, moved, total)
        z_out[t] = total
    first = rows_of((cx, 8, 128)) < EDGE
    for f in range(4):
        for c in range(3):
            q = 3 * f + c
            y_out[q * cx : (q + 1) * cx] = jnp.where(first, refs[f][c, :, 0:8], refs[f][c, :, 8:16])


def own_kernel(ip_in, e_in, h_in, y1, z_in, yz,
               a_out, b_out, c_out, e_out, sc_out, se_out, I, E, H):
    at = Place()
    cx = e_in.shape[1]
    lane = at.lane
    zero = jnp.zeros((24, 128), F32)
    strips = []
    for f, X, src in ((PERM, I, ip_in), (ELEC, E, e_in), (MAGN, H, h_in)):
        strip = []
        for c in range(3):
            q = 3 * f + c
            X[c, 0] = zero
            X[c, cx + 1] = zero
            X[c, 1 : cx + 1, 0:16] = src[c]
            X[c, 1 : cx + 1, 16:24] = at.y_part(y1[q * cx : (q + 1) * cx])
            if f == PERM:
                X[c] = time_step * X[c]
            got = jnp.concatenate([z_in[q // 4], at.y_part(yz[q // 4])], axis=0)
            tile = at.strip_own([X[c, x] for x in range(1, cx + 1)])
            tile = at.strip_got(tile, time_step * got if f == PERM else got, q)
            strip.append(tile)
        strips.append(tuple(strip))
    si, se, sh = strips

    def sx_up(v):
        return jnp.where(lane >= 112, 0.0, pltpu.roll(v, 112, 1))

    def sx_down(v):
        return jnp.where(lane < 16, 0.0, pltpu.roll(v, 16, 1))

    xs = list(range(1, cx + 1))
    up_strip, down_strip = zero, zero
    for n in range(STEPS):
        downs = get(E, 1, (1, 2))
        new = []
        for x in xs:
            curl = curl_f(get(E, x), get(E, x + 1, (1, 2)), y_up, at.z_up)
            keep = time_step * at.keep_row
            new.append(tuple(q - keep * v for q, v in zip(get(H, x), curl)))
        put(H, xs, new)
        curl = curl_f(se, (sx_up(se[1]), sx_up(se[2])), y_up, sz_up)
        down_from = se
        sh = tuple(q - time_step * at.keep_row * v for q, v in zip(sh, curl))
        ups = get(H, cx, (1, 2))
        new, curls = [], []
        for x in xs:
            curl = curl_b(get(H, x), get(H, x - 1, (1, 2)), y_down, at.z_down)
            new.append(tuple(q + i * v for q, i, v in zip(get(E, x), get(I, x), curl)))
            curls.append(curl)
        put(E, xs, new)
        for x, curl in zip(xs, curls):
            for c in range(3):
                c_out[n, c, x - 1] = curl[c][0:16]
        curl = curl_b(sh, (sx_down(sh[1]), sx_down(sh[2])), y_down, sz_down)
        se = tuple(q + i * v for q, i, v in zip(se, si, curl))
        for c in range(3):
            sc_out[n, c] = curl[c]
        for k in range(2):
            i = 2 * n + k
            a_out[i] = jnp.where(at.even, ups[k], downs[k])
            b_out[i] = jnp.where(at.even, downs[k], ups[k])
            here = lane // 16 == i
            up_strip = jnp.where(here, pltpu.roll(sh[1 + k], (16 * i + 16) % 128, 1), up_strip)
            down_strip = jnp.where(here, pltpu.roll(down_from[1 + k], 16 * i, 1), down_strip)
    edges = [jnp.concatenate([z_in[t], at.y_part(yz[t])], axis=0) for t in range(2)]
    up_edges = jnp.where(lane < 64, pltpu.roll(edges[0], 64, 1), edges[1])
    down_edges = jnp.where(lane < 64, edges[0], pltpu.roll(edges[1], 64, 1))
    a_out[N_TRACES + 1] = jnp.where(at.even, up_edges, down_edges)
    b_out[N_TRACES + 1] = jnp.where(at.even, down_edges, up_edges)
    a_out[N_TRACES] = jnp.where(at.even, up_strip, down_strip)
    b_out[N_TRACES] = jnp.where(at.even, down_strip, up_strip)
    for c in range(3):
        e_out[c] = E[c, 1 : cx + 1, 0:16]
    sput(se_out, se)


def adjoint_kernel(ip_in, sd_in, a_in, b_in, z_in, y1, yz, y2, c_own,
                   i_out, s_out, p_out, g_out, I, W, M, PS):
    at = Place()
    cx = ip_in.shape[1]
    lane = at.lane
    last = cx + 2 * DEEP
    top = STEPS - 1
    a_base = jnp.where(at.even, DEEP + cx, 0)
    b_base = jnp.where(at.even, 0, DEEP + cx)
    for f, X, src in ((PERM, I, ip_in), (SEED, PS.at[top], sd_in)):
        for c in range(3):
            q = 3 * f + c
            off = DEEP * q
            X[c, last] = jnp.zeros((24, 128), F32)
            X[c, DEEP : DEEP + cx, 0:16] = src[c]
            X[c, DEEP : DEEP + cx, 16:24] = at.y_part(y1[q * cx : (q + 1) * cx])
            X[c, pl.ds(a_base, DEEP), 0:16] = a_in[off : off + DEEP]
            X[c, pl.ds(a_base, DEEP), 16:24] = at.y_part(y2[off : off + DEEP])
            X[c, pl.ds(b_base, DEEP), 0:16] = b_in[off : off + DEEP]
            X[c, pl.ds(b_base, DEEP), 16:24] = at.y_part(y2[N_SLOTS + off : N_SLOTS + off + DEEP])
    for f, X in ((PERM, I), (SEED, PS.at[top])):
        for c in range(3):
            q = 3 * f + c
            t = q // 4
            own = jnp.concatenate([z_in[t], at.y_part(yz[t])], axis=0)
            around = [X[c, DEEP + cx + k] for k in range(DEEP)] + [jnp.zeros((24, 128), F32)] * 2
            around += [X[c, k] for k in range(DEEP)]
            s_out[q, :, 0:128] = at.strip_got(at.strip_own([X[c, DEEP + x] for x in range(cx)]), own, q)
            s_out[q, :, 128:256] = at.strip_own(around)

    def keep_at(x):
        return at.keep_row * jnp.where(at.no_low_x, 0.0, 1.0) if x < DEEP else at.keep_row

    def sweep(lo, hi, body):
        for first in range(lo, hi, 8):
            body(list(range(first, min(first + 8, hi))))

    def halve(xs):
        new = []
        for x in xs:
            half = tuple(time_step * v for v in get(I, x))
            new.append((half, tuple(a * b for a, b in zip(half, get(PS.at[top], x)))))
        put(I, xs, [n[0] for n in new])
        put(W, xs, [n[1] for n in new])

    sweep(0, last, halve)
    for c in range(3):
        W[c, last] = jnp.zeros((24, 128), F32)
        i_out[c] = I[c, 1 : 1 + i_out.shape[1]]

    for m in range(STEPS - 1):
        n = top - m

        def magnetic(xs, m=m):
            new = []
            for x in xs:
                curl = curl_f(get(W, x), get(W, x + 1, (1, 2)), y_up, at.z_up)
                keep = keep_at(x)
                if m == 0:
                    new.append(tuple(keep * v for v in curl))
                else:
                    new.append(tuple(q + keep * v for q, v in zip(get(M, x), curl)))
            put(M, xs, new)

        def electric(xs, m=m, n=n):
            new = []
            for x in xs:
                curl = curl_b(get(M, x), get(M, x - 1, (1, 2)), y_down, at.z_down)
                p = tuple(q - time_step * v for q, v in zip(get(PS.at[n], x), curl))
                new.append((p, tuple(a * b for a, b in zip(get(I, x), p))))
            put(PS.at[n - 1], xs, [v[0] for v in new])
            if m < STEPS - 2:
                put(W, xs, [v[1] for v in new])

        sweep(m, last - 1 - m, magnetic)
        sweep(m + 1, last - 1 - m, electric)

    for c in range(3):
        for x in range(cx):
            g = jnp.zeros((16, 128), F32)
            for n in range(STEPS):
                p = PS[n, c, DEEP + x, 0:16]
                g = g + p * c_own[n, c, x]
                if n < top:
                    p_out[n, c, x] = p
            g_out[c, x] = g


LOW_H = ([-1], [-2, -1, 0], [-2, -1, 0, 1], [-1, 0, 1, 2])
LOW_E = ([-1, 0], [-2, -1, 0, 1], [-1, 0, 1, 2], [0, 1, 2, 3])
HIGH_H = ([-1], [-2, -1, 0], [-3, -2, -1, 0], [-4, -3, -2, -1])
HIGH_E = ([-1, 0], [-2, -1, 0, 1], [-3, -2, -1, 0], [-4, -3, -2, -1])


def driven_kernel(sd_in, a_sent, b_sent, high_in, low_in, e_own, sc_own, se_own, i_in, s_in, p_in, g_own, ids,
                  e_out, se_out, s_out, E, H, G):
    at = Place()
    cx = e_own.shape[1]
    lane = at.lane
    base = 3
    zero = jnp.zeros((24, 128), F32)
    for c in range(3):
        for x in range(E.shape[1]):
            E[c, x] = zero
            H[c, x] = zero
        G[c] = g_own[c]

    def traces(a, b, i):
        return jnp.where(at.even, a[i], b[i])

    def upper(i):
        return high_in[i]

    def lower(i):
        return low_in[i]

    def own_up(i):
        return traces(a_sent, b_sent, i)

    def own_down(i):
        return traces(b_sent, a_sent, i)

    s_upper, s_lower, s_own_up, s_own_down = (t(N_TRACES) for t in (upper, lower, own_up, own_down))
    s_shape = (24, 256)
    s_keep = jnp.where((rows_of(s_shape) >= 20) & at.no_low_y, 0.0, time_step)
    s_keep = jnp.where((lanes_of(s_shape) >= 192) & at.no_low_x, 0.0, s_keep)

    def source(first, second, i, group):
        tiles = [pltpu.roll(v, (16 * (group - i)) % 128, 1) for v in (first, second)]
        return jnp.concatenate([jnp.where(lane // 16 == group, v, 0.0) for v in tiles], axis=1)

    above, below = upper(N_TRACES + 1), lower(N_TRACES + 1)
    edges = (
        jnp.where(lane < 64, above, pltpu.roll(below, 64, 1)),
        jnp.where(lane < 64, pltpu.roll(above, 64, 1), below),
    )
    strips = []
    for q in range(6):
        tile = at.strip_got(s_in[q, :, 128:256], edges[q // 4], q)
        strips.append(jnp.concatenate([s_in[q, :, 0:128], tile], axis=1))
    si = tuple(time_step * v for v in strips[0:3])
    sp = tuple(strips[3:6])
    adjoint = [None] * (STEPS - 1) + [sp]
    sm = (0.0, 0.0, 0.0)
    for n in range(STEPS - 1, 0, -1):
        sw = tuple(a * b for a, b in zip(si, sp))
        curl = curl_f(sw, [pltpu.roll(v, 240, 1) for v in sw[1:]], y_up, sz_up)
        sm = tuple(q + 2.0 * s_keep * v for q, v in zip(sm, curl))
        curl = curl_b(sm, [pltpu.roll(v, 16, 1) for v in sm[1:]], y_down, sz_down)
        sp = tuple(q - time_step * v for q, v in zip(sp, curl))
        adjoint[n - 1] = sp

    se = sh = (jnp.zeros(s_shape, F32),) * 3
    sg = (0.0, 0.0, 0.0)
    for n in range(STEPS):
        xs = LOW_H[n] + [cx + x for x in HIGH_H[n]]
        new = []
        for x in xs:
            nxt = get(E, base + x + 1, (1, 2))
            if x == -1:
                nxt = tuple(v + own_down(2 * n + k) for k, v in enumerate(nxt))
            if x == cx - 1:
                nxt = tuple(v + upper(2 * n + k) for k, v in enumerate(nxt))
            curl = curl_f(get(E, base + x), nxt, y_up, at.z_up)
            keep = time_step * at.keep_row
            if x < 0:
                keep = keep * jnp.where(at.no_low_x, 0.0, 1.0)
            new.append(tuple(q - keep * v for q, v in zip(get(H, base + x), curl)))
        put(H, [base + x for x in xs], new)
        nxt = tuple(pltpu.roll(se[1 + k], 240, 1) + source(s_upper, s_own_down, 2 * n + k, 7) for k in range(2))
        curl = curl_f(se, nxt, y_up, sz_up)
        sh = tuple(q - s_keep * v for q, v in zip(sh, curl))

        xs = LOW_E[n] + [cx + x for x in HIGH_E[n]]
        new, grads = [], []
        for x in xs:
            prv = get(H, base + x - 1, (1, 2))
            if x == 0:
                prv = tuple(v + lower(2 * n + k) for k, v in enumerate(prv))
            if x == cx:
                prv = tuple(v + own_up(2 * n + k) for k, v in enumerate(prv))
            curl = curl_b(get(H, base + x), prv, y_down, at.z_down)
            new.append(tuple(q + i * v for q, i, v in zip(get(E, base + x), get(i_in, 2 + x), curl)))
            grads.append(curl)
        put(E, [base + x for x in xs], new)
        for x, curl in zip(xs, grads):
            if 0 <= x < cx:
                for c in range(3):
                    p = sd_in[c, x] if n == STEPS - 1 else p_in[n, c, x]
                    G[c, x] += p * curl[c][0:16]
        prv = tuple(pltpu.roll(sh[1 + k], 16, 1) + source(s_lower, s_own_up, 2 * n + k, 0) for k in range(2))
        curl = curl_b(sh, prv, y_down, sz_down)
        se = tuple(q + i * v for q, i, v in zip(se, si, curl))
        sg = tuple(
            g + adjoint[n][c][:, 0:128] * (curl[c][:, 0:128] + sc_own[n, c]) for c, g in enumerate(sg)
        )

    for c in range(3):
        se_out[c] = se[c][0:16, 0:128] + se_own[c, 0:16]
        e_out[c] = E[c, base : base + cx, 0:16] + e_own[c]
    s_grad = [sg[c][0:16] for c in range(3)]

    acc = jnp.zeros((80, 128), F32)
    for x in range(cx):
        grads = []
        for c in range(3):
            grads.append(at.with_seam(G[c, x], s_grad[c], x))
        lhs, rhs = [], []
        for r in range(2):
            g = jnp.concatenate([v[8 * r : 8 * r + 8] for v in grads], axis=0)
            one = g.astype(jnp.bfloat16).astype(F32)
            rest = g - one
            two = rest.astype(jnp.bfloat16).astype(F32)
            three = rest - two
            lhs.append(jnp.concatenate([one, two, three, jnp.zeros((8, 128), F32)], axis=0).astype(jnp.bfloat16))
            region = ids[x, 8 * r : 8 * r + 8]
            slot = jnp.where(
                region < at.second_owner * REG_DEV,
                region - at.first_owner * REG_DEV,
                region - at.second_owner * REG_DEV + REG_DEV,
            )
            hot = jnp.concatenate([jnp.where(slot == s, 1.0, 0.0) for s in range(2 * REG_DEV)], axis=0)
            rhs.append(hot.astype(jnp.bfloat16))
        acc = acc + lax.dot_general(
            jnp.concatenate(lhs, axis=1),
            jnp.concatenate(rhs, axis=1),
            (((1,), (1,)), ((), ())),
            preferred_element_type=F32,
        )
    sums = acc[0:24] + acc[24:48] + acc[48:72]
    sums = jnp.where(rows_of((24, 128)) % 8 == lanes_of((24, 128)) % 8, sums, 0.0)
    parts = [jnp.sum(sums[8 * c : 8 * c + 8], axis=0, keepdims=True) for c in range(3)]
    parts = jnp.concatenate(parts + [jnp.zeros((5, 128), F32)], axis=0)
    fold = jnp.where(rows_of((128, 128)) // 8 == lanes_of((128, 128)), time_step * grad_scale, 0.0)
    s_out[...] = jnp.dot(parts, fold, precision=lax.Precision.HIGHEST, preferred_element_type=F32)


def last_kernel(ip_in, sd_in, a_got, b_got, z_in, y1, yz, y2, c_own, a_sent, b_sent, a_in, b_in, e_own, sc_own, se_own, ids,
                e_out, se_out, s_out, I, W, M, PS, E, H, G, i_ext, s_ext, p_own, g_own):
    adjoint_kernel(ip_in, sd_in, a_got, b_got, z_in, y1, yz, y2, c_own, i_ext, s_ext, p_own, g_own, I, W, M, PS)
    driven_kernel(sd_in, a_sent, b_sent, a_in, b_in, e_own, sc_own, se_own, i_ext, s_ext, p_own, g_own, ids,
                  e_out, se_out, s_out, E, H, G)


def finish_kernel(e_in, se_in, e_out):
    at = Place()
    for c in range(3):
        for x in range(e_in.shape[1]):
            e_out[c, x] = at.with_seam(e_in[c, x], se_in[c], x)


def y_rows(v):
    first = lax.broadcasted_iota(jnp.int32, (1, 8, 1), 1) < EDGE
    return jnp.where(first, v[:, 0:8], v[:, 8:16])


def local(e_start, h_start, inv_perm, adj_seed, region_ids):
    n_gx, n_gy = lax.axis_size("gx"), lax.axis_size("gy")
    xi = lax.axis_index("gx")
    cx = e_start.shape[1]
    even = (xi + 1) % 2
    vmem = pl.BlockSpec(memory_space=pltpu.VMEM)
    shape = lambda *dims: jax.ShapeDtypeStruct(dims, F32)
    tile = lambda *dims: pltpu.VMEM(dims, F32)

    a_pairs = [(i, i ^ 1) for i in range(n_gx)]
    b_pairs = [(i, ((i - 1) ^ 1) + 1) for i in range(1, n_gx - 1)]

    def swap_y(v):
        if n_gy == 2:
            return lax.ppermute(v, "gy", [(0, 1), (1, 0)])
        up = lax.ppermute(v, "gy", [(i, i + 1) for i in range(n_gy - 1)])
        down = lax.ppermute(v, "gy", [(i + 1, i) for i in range(n_gy - 1)])
        first = lax.broadcasted_iota(jnp.int32, (1, 8, 1), 1) < EDGE
        return jnp.where(first, down, up)

    def call(kernel, outs, scratch, args, mib, specs=None, cost=None):
        return pl.pallas_call(
            kernel,
            out_shape=outs,
            in_specs=specs or [vmem] * len(args),
            out_specs=(vmem,) * len(outs),
            scratch_shapes=scratch,
            cost_estimate=cost,
            compiler_params=pltpu.CompilerParams(vmem_limit_bytes=mib * 1024 * 1024),
        )(*args)

    own = tile(*e_start.shape)
    a_msg, b_msg, z_msg, y_msg = call(
        pack_kernel,
        (shape(N_SLOTS, 16, 128), shape(N_SLOTS, 16, 128), shape(3, 16, 128), shape(12 * cx, 8, 128)),
        [own] * 4 + [pltpu.SemaphoreType.DMA((4,))],
        tuple(pltpu.with_memory_space_constraint(v, pltpu.HBM) for v in (inv_perm, adj_seed, e_start, h_start)),
        8,
        [pl.BlockSpec(memory_space=pltpu.HBM)] * 4,
    )
    z_got = lax.ppermute(z_msg, "gz", [(0, 1), (1, 0)])
    y1 = swap_y(y_msg)
    a_got = lax.ppermute(a_msg, "gx", a_pairs)
    b_got = lax.ppermute(b_msg, "gx", b_pairs)
    yz = swap_y(y_rows(z_got))

    n_msg = N_TRACES + 2
    field = tile(3, cx + 2, 24, 128)
    a_sent, b_sent, c_own, e_own, sc_own, se_own = call(
        own_kernel,
        (
            shape(n_msg, 24, 128),
            shape(n_msg, 24, 128),
            shape(STEPS, 3, cx, 16, 128),
            shape(3, cx, 16, 128),
            shape(STEPS, 3, 24, 128),
            shape(3, 24, 128),
        ),
        [field] * 3,
        (inv_perm, e_start, h_start, y1, z_got, yz),
        8,
    )
    a_in = lax.ppermute(a_sent, "gx", a_pairs)
    b_in = lax.ppermute(b_sent, "gx", b_pairs)
    a_got, b_got, _ = lax.optimization_barrier((a_got, b_got, a_sent))
    high_in = jnp.where(even == 1, a_in, b_in)
    low_in = jnp.where(even == 1, b_in, a_in)
    y2 = swap_y(jnp.concatenate([y_rows(v) for v in (a_got, b_got)], axis=0))

    planes = cx + 2 * DEEP + 1
    field = tile(3, planes, 24, 128)
    driven = tile(3, cx + 5, 24, 128)
    e_main, e_strip, sums = call(
        last_kernel,
        (shape(*e_start.shape), shape(3, 16, 128), shape(8, 128)),
        [field] * 3
        + [tile(STEPS, 3, planes, 24, 128)]
        + [driven] * 2
        + [own, tile(3, cx + 4, 24, 128), tile(6, 24, 256), tile(STEPS - 1, 3, cx, 16, 128), own],
        (inv_perm, adj_seed, a_got, b_got, z_got, y1, yz, y2, c_own, a_sent, b_sent, high_in, low_in, e_own, sc_own, se_own, region_ids),
        16,
    )
    (e_field,) = call(finish_kernel, (shape(*e_start.shape),), [], (e_main, e_strip), 4)
    total = sums + lax.ppermute(sums, "gx", a_pairs)
    owned = jnp.where(even == 1, total[0:3, 0:REG_DEV], total[0:3, REG_DEV : 2 * REG_DEV])
    return e_field, owned


def solution(mesh):
    placed = (
        P(None, "gx", "gy", "gz"),
        P(None, "gx", "gy", "gz"),
        P(None, "gx", "gy", "gz"),
        P(None, "gx", "gy", "gz"),
        P("gx", "gy", "gz"),
    )
    return jax.shard_map(
        local,
        mesh=mesh,
        in_specs=placed,
        out_specs=(P(None, "gx", "gy", "gz"), P(None, ("gx", "gy", "gz"))),
        check_vma=False,
    )
```

```python
import jax
import jax.numpy as jnp
from jax import lax
from jax.experimental import pallas as pl
from jax.experimental.pallas import tpu as pltpu
from jax.sharding import PartitionSpec as P

STEPS = 4
REG_DEV = 8
DEEP = 3
EDGE = 4
PERM, SEED, ELEC, MAGN = range(4)
N_SLOTS = 2 * 3 * DEEP
N_TRACES = 2 * STEPS
GROUP = 2

time_step = 0.5
grad_scale = 1.0 / 64.0
F32 = jnp.float32


def lanes_of(shape):
    return lax.broadcasted_iota(jnp.int32, shape, len(shape) - 1)


def rows_of(shape):
    return lax.broadcasted_iota(jnp.int32, shape, len(shape) - 2)


def roll_up(v, axis):
    return pltpu.roll(v, v.shape[axis] - 1, axis)


def roll_down(v, axis):
    return pltpu.roll(v, 1, axis)


def curl_f(v, nxt, shift_y, shift_z):
    vx, vy, vz = v
    ny, nz = nxt
    return (
        (shift_y(vz) - vz) - (shift_z(vy) - vy),
        (shift_z(vx) - vx) - (nz - vz),
        (ny - vy) - (shift_y(vx) - vx),
    )


def curl_b(v, prv, shift_y, shift_z):
    vx, vy, vz = v
    py, pz = prv
    return (
        (vz - shift_y(vz)) - (vy - shift_z(vy)),
        (vx - shift_z(vx)) - (vz - pz),
        (vy - py) - (vx - shift_y(vx)),
    )


class Place:
    def __init__(self):
        xi, yi, self.gz = (lax.axis_index(a) for a in ("gx", "gy", "gz"))
        n_gy, n_gz = lax.axis_size("gy"), lax.axis_size("gz")
        even = (xi + 1) % 2
        self.even = even == 1
        self.no_low_x = xi == 0
        self.no_low_y = yi == 0
        self.no_high_y = yi == n_gy - 1
        own_flat = xi * n_gy * n_gz + yi * n_gz + self.gz
        self.first_owner = own_flat - (1 - even) * n_gy * n_gz
        self.second_owner = self.first_owner + n_gy * n_gz
        self.lane = lanes_of((24, 128))
        self.row = rows_of((24, 128))
        self.keep_row = jnp.where((self.row >= 20) & self.no_low_y, 0.0, 1.0)
        self.own_off = jnp.where(self.gz == 0, 8, 4)
        self.own_j = jnp.where(self.gz == 0, 0, 4)
        self.got_j = jnp.where(self.gz == 0, 8, 0)

    def y_part(self, v):
        high = jnp.where(self.no_high_y, 0.0, 1.0)
        low = jnp.where(self.no_low_y, 0.0, 1.0)
        return v * jnp.where(rows_of(v.shape[-2:]) < EDGE, high, low)

    def strip_own(self, planes):
        lane = self.lane
        acc = jnp.zeros((24, 128), F32)
        for x, plane in enumerate(planes):
            acc = jnp.where(lane // 16 == x, pltpu.roll(plane, (16 * x + self.own_off) % 128, 1), acc)
        j = lane % 16
        return jnp.where((j >= self.own_j) & (j < self.own_j + 8), acc, 0.0)

    def strip_got(self, tile, got, q):
        j = self.lane % 16
        got = pltpu.roll(got, (self.got_j - 4 * (q % 4) + 128) % 128, 1)
        return jnp.where((j >= self.got_j) & (j < self.got_j + EDGE), got, tile)

    def with_seam(self, plane, strip, x):
        lane = lanes_of((16, 128))
        lo = jnp.where(self.gz == 0, 128 - EDGE, 0)
        moved = pltpu.roll(strip, (lo - 16 * x - EDGE + 256) % 128, 1)
        return jnp.where((lane >= lo) & (lane < lo + EDGE), moved, plane)

    def z_up(self, v):
        return jnp.where(self.lane == 127, 0.0, roll_up(v, 1))

    def z_down(self, v):
        return jnp.where(self.lane == 0, 0.0, roll_down(v, 1))


def y_up(v):
    return roll_up(v, 0)


def y_down(v):
    return roll_down(v, 0)


def sz_up(v):
    return roll_up(v, 1)


def sz_down(v):
    return roll_down(v, 1)


def parts_of(xs):
    return [xs[i : i + GROUP] for i in range(0, len(xs), GROUP)]


def get(ref, x, comps=(0, 1, 2)):
    return tuple(ref[c, x] for c in comps)


def put(ref, xs, values):
    for x, v in zip(xs, values):
        for c in range(3):
            ref[c, x] = v[c]


def sget(ref):
    return tuple(ref[c] for c in range(3))


def sput(ref, v):
    for c in range(3):
        ref[c] = v[c]


def pack_kernel(ip_hbm, sd_hbm, e_hbm, h_hbm, a_out, b_out, z_out, y_out, ip, sd, e, h, sems):
    even, gz = (lax.axis_index("gx") + 1) % 2, lax.axis_index("gz")
    refs = (ip, sd, e, h)
    copies = []
    for i, src in enumerate((ip_hbm, sd_hbm, e_hbm, h_hbm)):
        copies.append(pltpu.make_async_copy(src, refs[i], sems.at[i]))
    for copy in copies:
        copy.start()
    for copy in copies:
        copy.wait()
    cx = e.shape[1]
    a_base = jnp.where(even == 1, cx - DEEP, 0)
    b_base = jnp.where(even == 1, 0, cx - DEEP)
    for f in (PERM, SEED):
        for c in range(3):
            off = DEEP * (3 * f + c)
            a_out[off : off + DEEP] = refs[f][c, pl.ds(a_base, DEEP)]
            b_out[off : off + DEEP] = refs[f][c, pl.ds(b_base, DEEP)]
    group = lanes_of((16, 128)) // EDGE
    z_off = jnp.where(gz == 0, EDGE, 0)
    for t in range(3):
        total = jnp.zeros((16, 128), F32)
        for k in range(4):
            f, c = divmod(4 * t + k, 3)
            for x in range(cx):
                moved = pltpu.roll(refs[f][c, x], (16 * x + 4 * k + z_off) % 128, 1)
                total = jnp.where(group == 4 * x + k, moved, total)
        z_out[t] = total
    first = rows_of((cx, 8, 128)) < EDGE
    for f in range(4):
        for c in range(3):
            q = 3 * f + c
            y_out[q * cx : (q + 1) * cx] = jnp.where(first, refs[f][c, :, 0:8], refs[f][c, :, 8:16])


def own_kernel(ip_in, e_in, h_in, y1, z_in, yz,
               a_out, b_out, c_out, e_out, sc_out, se_out, I, E, H):
    at = Place()
    cx = e_in.shape[1]
    lane = at.lane
    zero = jnp.zeros((24, 128), F32)
    strips = []
    for f, X, src in ((PERM, I, ip_in), (ELEC, E, e_in), (MAGN, H, h_in)):
        strip = []
        for c in range(3):
            q = 3 * f + c
            X[c, 0] = zero
            X[c, cx + 1] = zero
            X[c, 1 : cx + 1, 0:16] = src[c]
            X[c, 1 : cx + 1, 16:24] = at.y_part(y1[q * cx : (q + 1) * cx])
            if f == PERM:
                X[c] = time_step * X[c]
            got = jnp.concatenate([z_in[q // 4], at.y_part(yz[q // 4])], axis=0)
            tile = at.strip_own([X[c, x] for x in range(1, cx + 1)])
            tile = at.strip_got(tile, time_step * got if f == PERM else got, q)
            strip.append(tile)
        strips.append(tuple(strip))
    si, se, sh = strips

    def sx_up(v):
        return jnp.where(lane >= 112, 0.0, pltpu.roll(v, 112, 1))

    def sx_down(v):
        return jnp.where(lane < 16, 0.0, pltpu.roll(v, 16, 1))

    xs = list(range(1, cx + 1))
    up_strip, down_strip = zero, zero
    for n in range(STEPS):
        downs = get(E, 1, (1, 2))
        keep = time_step * at.keep_row
        for part in parts_of(xs):
            new = []
            for x in part:
                curl = curl_f(get(E, x), get(E, x + 1, (1, 2)), y_up, at.z_up)
                new.append(tuple(q - keep * v for q, v in zip(get(H, x), curl)))
            put(H, part, new)
        curl = curl_f(se, (sx_up(se[1]), sx_up(se[2])), y_up, sz_up)
        down_from = se
        sh = tuple(q - time_step * at.keep_row * v for q, v in zip(sh, curl))
        ups = get(H, cx, (1, 2))
        for part in parts_of(xs):
            new, curls = [], []
            for x in part:
                curl = curl_b(get(H, x), get(H, x - 1, (1, 2)), y_down, at.z_down)
                new.append(tuple(q + i * v for q, i, v in zip(get(E, x), get(I, x), curl)))
                curls.append(curl)
            put(E, part, new)
            for x, curl in zip(part, curls):
                for c in range(3):
                    c_out[n, c, x - 1] = curl[c][0:16]
        curl = curl_b(sh, (sx_down(sh[1]), sx_down(sh[2])), y_down, sz_down)
        se = tuple(q + i * v for q, i, v in zip(se, si, curl))
        for c in range(3):
            sc_out[n, c] = curl[c]
        for k in range(2):
            i = 2 * n + k
            a_out[i] = jnp.where(at.even, ups[k], downs[k])
            b_out[i] = jnp.where(at.even, downs[k], ups[k])
            here = lane // 16 == i
            up_strip = jnp.where(here, pltpu.roll(sh[1 + k], (16 * i + 16) % 128, 1), up_strip)
            down_strip = jnp.where(here, pltpu.roll(down_from[1 + k], 16 * i, 1), down_strip)
    edges = [jnp.concatenate([z_in[t], at.y_part(yz[t])], axis=0) for t in range(2)]
    up_edges = jnp.where(lane < 64, pltpu.roll(edges[0], 64, 1), edges[1])
    down_edges = jnp.where(lane < 64, edges[0], pltpu.roll(edges[1], 64, 1))
    a_out[N_TRACES + 1] = jnp.where(at.even, up_edges, down_edges)
    b_out[N_TRACES + 1] = jnp.where(at.even, down_edges, up_edges)
    a_out[N_TRACES] = jnp.where(at.even, up_strip, down_strip)
    b_out[N_TRACES] = jnp.where(at.even, down_strip, up_strip)
    for c in range(3):
        e_out[c] = E[c, 1 : cx + 1, 0:16]
    sput(se_out, se)


def adjoint_kernel(ip_in, sd_in, a_in, b_in, z_in, y1, yz, y2,
                   s_out, I, W, M, PS):
    at = Place()
    cx = ip_in.shape[1]
    lane = at.lane
    last = cx + 2 * DEEP
    top = STEPS - 1
    a_base = jnp.where(at.even, DEEP + cx, 0)
    b_base = jnp.where(at.even, 0, DEEP + cx)
    for f, X, src in ((PERM, I, ip_in), (SEED, PS.at[top], sd_in)):
        for c in range(3):
            q = 3 * f + c
            off = DEEP * q
            X[c, last] = jnp.zeros((24, 128), F32)
            X[c, DEEP : DEEP + cx, 0:16] = src[c]
            X[c, DEEP : DEEP + cx, 16:24] = at.y_part(y1[q * cx : (q + 1) * cx])
            X[c, pl.ds(a_base, DEEP), 0:16] = a_in[off : off + DEEP]
            X[c, pl.ds(a_base, DEEP), 16:24] = at.y_part(y2[off : off + DEEP])
            X[c, pl.ds(b_base, DEEP), 0:16] = b_in[off : off + DEEP]
            X[c, pl.ds(b_base, DEEP), 16:24] = at.y_part(y2[N_SLOTS + off : N_SLOTS + off + DEEP])
    for f, X in ((PERM, I), (SEED, PS.at[top])):
        for c in range(3):
            q = 3 * f + c
            t = q // 4
            own = jnp.concatenate([z_in[t], at.y_part(yz[t])], axis=0)
            around = [X[c, DEEP + cx + k] for k in range(DEEP)] + [jnp.zeros((24, 128), F32)] * 2
            around += [X[c, k] for k in range(DEEP)]
            s_out[q, :, 0:128] = at.strip_got(at.strip_own([X[c, DEEP + x] for x in range(cx)]), own, q)
            s_out[q, :, 128:256] = at.strip_own(around)

    def keep_at(x):
        return at.keep_row * jnp.where(at.no_low_x, 0.0, 1.0) if x < DEEP else at.keep_row

    def sweep(lo, hi, body):
        for first in range(lo, hi, GROUP):
            body(list(range(first, min(first + GROUP, hi))))

    def halve(xs):
        new = []
        for x in xs:
            half = tuple(time_step * v for v in get(I, x))
            new.append((half, tuple(a * b for a, b in zip(half, get(PS.at[top], x)))))
        put(I, xs, [n[0] for n in new])
        put(W, xs, [n[1] for n in new])

    sweep(0, last, halve)
    for c in range(3):
        W[c, last] = jnp.zeros((24, 128), F32)

    for m in range(STEPS - 1):
        n = top - m

        def magnetic(xs, m=m):
            new = []
            for x in xs:
                curl = curl_f(get(W, x), get(W, x + 1, (1, 2)), y_up, at.z_up)
                keep = keep_at(x)
                if m == 0:
                    new.append(tuple(keep * v for v in curl))
                else:
                    new.append(tuple(q + keep * v for q, v in zip(get(M, x), curl)))
            put(M, xs, new)

        def electric(xs, m=m, n=n):
            new = []
            for x in xs:
                curl = curl_b(get(M, x), get(M, x - 1, (1, 2)), y_down, at.z_down)
                p = tuple(q - time_step * v for q, v in zip(get(PS.at[n], x), curl))
                new.append((p, tuple(a * b for a, b in zip(get(I, x), p))))
            put(PS.at[n - 1], xs, [v[0] for v in new])
            if m < STEPS - 2:
                put(W, xs, [v[1] for v in new])

        yield
        sweep(m, last - 1 - m, magnetic)
        yield
        sweep(m + 1, last - 1 - m, electric)


LOW_H = ([-1], [-2, -1, 0], [-2, -1, 0, 1], [-1, 0, 1, 2])
LOW_E = ([-1, 0], [-2, -1, 0, 1], [-1, 0, 1, 2], [0, 1, 2, 3])
HIGH_H = ([-1], [-2, -1, 0], [-3, -2, -1, 0], [-4, -3, -2, -1])
HIGH_E = ([-1, 0], [-2, -1, 0, 1], [-3, -2, -1, 0], [-4, -3, -2, -1])


def driven_kernel(a_sent, b_sent, high_in, low_in, e_own, sc_own, se_own, s_in, I, e_out, se_out, sg_out, E, H, CD):
    at = Place()
    cx = e_own.shape[1]
    lane = at.lane
    base = 3
    zero = jnp.zeros((24, 128), F32)
    for c in range(3):
        for x in range(E.shape[1]):
            E[c, x] = zero
            H[c, x] = zero

    def traces(a, b, i):
        return jnp.where(at.even, a[i], b[i])

    def upper(i):
        return high_in[i]

    def lower(i):
        return low_in[i]

    def own_up(i):
        return traces(a_sent, b_sent, i)

    def own_down(i):
        return traces(b_sent, a_sent, i)

    s_upper, s_lower, s_own_up, s_own_down = (t(N_TRACES) for t in (upper, lower, own_up, own_down))
    s_shape = (24, 256)
    s_keep = jnp.where((rows_of(s_shape) >= 20) & at.no_low_y, 0.0, time_step)
    s_keep = jnp.where((lanes_of(s_shape) >= 192) & at.no_low_x, 0.0, s_keep)

    def source(first, second, i, group):
        tiles = [pltpu.roll(v, (16 * (group - i)) % 128, 1) for v in (first, second)]
        return jnp.concatenate([jnp.where(lane // 16 == group, v, 0.0) for v in tiles], axis=1)

    above, below = upper(N_TRACES + 1), lower(N_TRACES + 1)
    edges = (
        jnp.where(lane < 64, above, pltpu.roll(below, 64, 1)),
        jnp.where(lane < 64, pltpu.roll(above, 64, 1), below),
    )
    strips = []
    for q in range(6):
        tile = at.strip_got(s_in[q, :, 128:256], edges[q // 4], q)
        strips.append(jnp.concatenate([s_in[q, :, 0:128], tile], axis=1))
    si = tuple(time_step * v for v in strips[0:3])
    sp = tuple(strips[3:6])
    adjoint = [None] * (STEPS - 1) + [sp]
    sm = (0.0, 0.0, 0.0)
    s_curls = []
    se = sh = (jnp.zeros(s_shape, F32),) * 3
    for n in range(STEPS):
        yield
        xs = LOW_H[n] + [cx + x for x in HIGH_H[n]]
        for part in parts_of(xs):
            new = []
            for x in part:
                nxt = get(E, base + x + 1, (1, 2))
                if x == -1:
                    nxt = tuple(v + own_down(2 * n + k) for k, v in enumerate(nxt))
                if x == cx - 1:
                    nxt = tuple(v + upper(2 * n + k) for k, v in enumerate(nxt))
                curl = curl_f(get(E, base + x), nxt, y_up, at.z_up)
                keep = time_step * at.keep_row
                if x < 0:
                    keep = keep * jnp.where(at.no_low_x, 0.0, 1.0)
                new.append(tuple(q - keep * v for q, v in zip(get(H, base + x), curl)))
            put(H, [base + x for x in part], new)
        nxt = tuple(pltpu.roll(se[1 + k], 240, 1) + source(s_upper, s_own_down, 2 * n + k, 7) for k in range(2))
        curl = curl_f(se, nxt, y_up, sz_up)
        sh = tuple(q - s_keep * v for q, v in zip(sh, curl))
        if n < STEPS - 1:
            sw = tuple(a * b for a, b in zip(si, sp))
            curl = curl_f(sw, [pltpu.roll(v, 240, 1) for v in sw[1:]], y_up, sz_up)
            sm = tuple(q + 2.0 * s_keep * v for q, v in zip(sm, curl))

        yield
        xs = LOW_E[n] + [cx + x for x in HIGH_E[n]]
        for part in parts_of(xs):
            new, grads = [], []
            for x in part:
                prv = get(H, base + x - 1, (1, 2))
                if x == 0:
                    prv = tuple(v + lower(2 * n + k) for k, v in enumerate(prv))
                if x == cx:
                    prv = tuple(v + own_up(2 * n + k) for k, v in enumerate(prv))
                curl = curl_b(get(H, base + x), prv, y_down, at.z_down)
                new.append(tuple(q + i * v for q, i, v in zip(get(E, base + x), get(I, DEEP + x), curl)))
                grads.append(curl)
            put(E, [base + x for x in part], new)
            for x, curl in zip(part, grads):
                if 0 <= x < cx:
                    for c in range(3):
                        CD[n, c, x] = curl[c][0:16]
        prv = tuple(pltpu.roll(sh[1 + k], 16, 1) + source(s_lower, s_own_up, 2 * n + k, 0) for k in range(2))
        curl = curl_b(sh, prv, y_down, sz_down)
        se = tuple(q + i * v for q, i, v in zip(se, si, curl))
        s_curls.append(tuple(v[:, 0:128] for v in curl))
        if n < STEPS - 1:
            curl = curl_b(sm, [pltpu.roll(v, 16, 1) for v in sm[1:]], y_down, sz_down)
            sp = tuple(q - time_step * v for q, v in zip(sp, curl))
            adjoint[STEPS - 2 - n] = sp
    for c in range(3):
        se_out[c] = se[c][0:16, 0:128] + se_own[c, 0:16]
        e_out[c] = E[c, base : base + cx, 0:16] + e_own[c]
        sg_out[c] = sum(adjoint[n][c][0:16, 0:128] * (s_curls[n][c] + sc_own[n, c])[0:16] for n in range(STEPS))
    yield


def sums_kernel(PS, c_own, CD, sg, ids, s_out):
    at = Place()
    cx = ids.shape[0]
    acc = jnp.zeros((80, 128), F32)
    for x in range(cx):
        grads = []
        for c in range(3):
            g = 0.0
            for n in range(STEPS):
                curl = c_own[n, c, x]
                if x in LOW_E[n] or x - cx in HIGH_E[n]:
                    curl = curl + CD[n, c, x]
                g = g + PS[n, c, DEEP + x, 0:16] * curl
            grads.append(at.with_seam(g, sg[c], x))
        lhs, rhs = [], []
        for r in range(2):
            g = jnp.concatenate([v[8 * r : 8 * r + 8] for v in grads], axis=0)
            one = g.astype(jnp.bfloat16).astype(F32)
            rest = g - one
            two = rest.astype(jnp.bfloat16).astype(F32)
            three = rest - two
            lhs.append(jnp.concatenate([one, two, three, jnp.zeros((8, 128), F32)], axis=0).astype(jnp.bfloat16))
            region = ids[x, 8 * r : 8 * r + 8]
            slot = jnp.where(
                region < at.second_owner * REG_DEV,
                region - at.first_owner * REG_DEV,
                region - at.second_owner * REG_DEV + REG_DEV,
            )
            hot = jnp.concatenate([jnp.where(slot == s, 1.0, 0.0) for s in range(2 * REG_DEV)], axis=0)
            rhs.append(hot.astype(jnp.bfloat16))
        acc = acc + lax.dot_general(
            jnp.concatenate(lhs, axis=1),
            jnp.concatenate(rhs, axis=1),
            (((1,), (1,)), ((), ())),
            preferred_element_type=F32,
        )
    sums = acc[0:24] + acc[24:48] + acc[48:72]
    sums = jnp.where(rows_of((24, 128)) % 8 == lanes_of((24, 128)) % 8, sums, 0.0)
    parts = [jnp.sum(sums[8 * c : 8 * c + 8], axis=0, keepdims=True) for c in range(3)]
    parts = jnp.concatenate(parts + [jnp.zeros((5, 128), F32)], axis=0)
    fold = jnp.where(rows_of((128, 128)) // 8 == lanes_of((128, 128)), time_step * grad_scale, 0.0)
    s_out[...] = jnp.dot(parts, fold, precision=lax.Precision.HIGHEST, preferred_element_type=F32)


def last_kernel(ip_in, sd_in, a_got, b_got, z_in, y1, yz, y2, c_own, a_sent, b_sent, high_in, low_in, e_own, sc_own, se_own, ids,
                e_out, se_out, s_out, I, W, M, PS, E, H, CD, s_ext, sg):
    runs = (
        adjoint_kernel(ip_in, sd_in, a_got, b_got, z_in, y1, yz, y2, s_ext, I, W, M, PS),
        driven_kernel(a_sent, b_sent, high_in, low_in, e_own, sc_own, se_own, s_ext, I, e_out, se_out, sg, E, H, CD),
    )
    for _ in range(2 * STEPS + 1):
        for run in runs:
            next(run, None)
    sums_kernel(PS, c_own, CD, sg, ids, s_out)


def finish_kernel(e_in, se_in, e_out):
    at = Place()
    for c in range(3):
        for x in range(e_in.shape[1]):
            e_out[c, x] = at.with_seam(e_in[c, x], se_in[c], x)


def y_rows(v):
    first = lax.broadcasted_iota(jnp.int32, (1, 8, 1), 1) < EDGE
    return jnp.where(first, v[:, 0:8], v[:, 8:16])


def local(e_start, h_start, inv_perm, adj_seed, region_ids):
    n_gx, n_gy = lax.axis_size("gx"), lax.axis_size("gy")
    xi = lax.axis_index("gx")
    cx = e_start.shape[1]
    even = (xi + 1) % 2
    vmem = pl.BlockSpec(memory_space=pltpu.VMEM)
    shape = lambda *dims: jax.ShapeDtypeStruct(dims, F32)
    tile = lambda *dims: pltpu.VMEM(dims, F32)

    a_pairs = [(i, i ^ 1) for i in range(n_gx)]
    b_pairs = [(i, ((i - 1) ^ 1) + 1) for i in range(1, n_gx - 1)]

    def swap_y(v):
        if n_gy == 2:
            return lax.ppermute(v, "gy", [(0, 1), (1, 0)])
        up = lax.ppermute(v, "gy", [(i, i + 1) for i in range(n_gy - 1)])
        down = lax.ppermute(v, "gy", [(i + 1, i) for i in range(n_gy - 1)])
        first = lax.broadcasted_iota(jnp.int32, (1, 8, 1), 1) < EDGE
        return jnp.where(first, down, up)

    def call(kernel, outs, scratch, args, mib, specs=None, cost=None):
        return pl.pallas_call(
            kernel,
            out_shape=outs,
            in_specs=specs or [vmem] * len(args),
            out_specs=(vmem,) * len(outs),
            scratch_shapes=scratch,
            cost_estimate=cost,
            compiler_params=pltpu.CompilerParams(vmem_limit_bytes=mib * 1024 * 1024),
        )(*args)

    own = tile(*e_start.shape)
    a_msg, b_msg, z_msg, y_msg = call(
        pack_kernel,
        (shape(N_SLOTS, 16, 128), shape(N_SLOTS, 16, 128), shape(3, 16, 128), shape(12 * cx, 8, 128)),
        [own] * 4 + [pltpu.SemaphoreType.DMA((4,))],
        tuple(pltpu.with_memory_space_constraint(v, pltpu.HBM) for v in (inv_perm, adj_seed, e_start, h_start)),
        8,
        [pl.BlockSpec(memory_space=pltpu.HBM)] * 4,
    )
    z_got = lax.ppermute(z_msg, "gz", [(0, 1), (1, 0)])
    y1 = swap_y(y_msg)
    a_got = lax.ppermute(a_msg, "gx", a_pairs)
    b_got = lax.ppermute(b_msg, "gx", b_pairs)
    yz = swap_y(y_rows(z_got))

    n_msg = N_TRACES + 2
    field = tile(3, cx + 2, 24, 128)
    a_sent, b_sent, c_own, e_own, sc_own, se_own = call(
        own_kernel,
        (
            shape(n_msg, 24, 128),
            shape(n_msg, 24, 128),
            shape(STEPS, 3, cx, 16, 128),
            shape(3, cx, 16, 128),
            shape(STEPS, 3, 24, 128),
            shape(3, 24, 128),
        ),
        [field] * 3,
        (inv_perm, e_start, h_start, y1, z_got, yz),
        8,
    )
    a_in = lax.ppermute(a_sent, "gx", a_pairs)
    b_in = lax.ppermute(b_sent, "gx", b_pairs)
    high_in = jnp.where(even == 1, a_in, b_in)
    low_in = jnp.where(even == 1, b_in, a_in)
    y2 = swap_y(jnp.concatenate([y_rows(v) for v in (a_got, b_got)], axis=0))

    planes = cx + 2 * DEEP + 1
    field = tile(3, planes, 24, 128)
    driven = tile(3, cx + 5, 24, 128)
    e_main, e_strip, sums = call(
        last_kernel,
        (shape(*e_start.shape), shape(3, 16, 128), shape(8, 128)),
        [field] * 3
        + [tile(STEPS, 3, planes, 24, 128)]
        + [driven] * 2
        + [tile(STEPS, 3, cx, 16, 128), tile(6, 24, 256), tile(3, 16, 128)],
        (inv_perm, adj_seed, a_got, b_got, z_got, y1, yz, y2, c_own, a_sent, b_sent, high_in, low_in, e_own, sc_own, se_own, region_ids),
        16,
    )
    (e_field,) = call(finish_kernel, (shape(*e_start.shape),), [], (e_main, e_strip), 4)
    total = sums + lax.ppermute(sums, "gx", a_pairs)
    owned = jnp.where(even == 1, total[0:3, 0:REG_DEV], total[0:3, REG_DEV : 2 * REG_DEV])
    return e_field, owned


def solution(mesh):
    placed = (
        P(None, "gx", "gy", "gz"),
        P(None, "gx", "gy", "gz"),
        P(None, "gx", "gy", "gz"),
        P(None, "gx", "gy", "gz"),
        P("gx", "gy", "gz"),
    )
    return jax.shard_map(
        local,
        mesh=mesh,
        in_specs=placed,
        out_specs=(P(None, "gx", "gy", "gz"), P(None, ("gx", "gy", "gz"))),
        check_vma=False,
    )
```

```python
import jax
import jax.numpy as jnp
from jax import lax
from jax.experimental import pallas as pl
from jax.experimental.pallas import tpu as pltpu
from jax.sharding import PartitionSpec as P

STEPS = 4
REG_DEV = 8
DEEP = 3
EDGE = 4
PERM, SEED, ELEC, MAGN = range(4)
N_SLOTS = 2 * 3 * DEEP
N_TRACES = 2 * STEPS
GROUP = 2

time_step = 0.5
grad_scale = 1.0 / 64.0
F32 = jnp.float32


def lanes_of(shape):
    return lax.broadcasted_iota(jnp.int32, shape, len(shape) - 1)


def rows_of(shape):
    return lax.broadcasted_iota(jnp.int32, shape, len(shape) - 2)


def roll_up(v, axis):
    return pltpu.roll(v, v.shape[axis] - 1, axis)


def roll_down(v, axis):
    return pltpu.roll(v, 1, axis)


def curl_f(v, nxt, shift_y, shift_z):
    vx, vy, vz = v
    ny, nz = nxt
    return (
        (shift_y(vz) - vz) - (shift_z(vy) - vy),
        (shift_z(vx) - vx) - (nz - vz),
        (ny - vy) - (shift_y(vx) - vx),
    )


def curl_b(v, prv, shift_y, shift_z):
    vx, vy, vz = v
    py, pz = prv
    return (
        (vz - shift_y(vz)) - (vy - shift_z(vy)),
        (vx - shift_z(vx)) - (vz - pz),
        (vy - py) - (vx - shift_y(vx)),
    )


class Place:
    def __init__(self):
        xi, yi, self.gz = (lax.axis_index(a) for a in ("gx", "gy", "gz"))
        n_gy, n_gz = lax.axis_size("gy"), lax.axis_size("gz")
        even = (xi + 1) % 2
        self.even = even == 1
        self.no_low_x = xi == 0
        self.no_low_y = yi == 0
        self.no_high_y = yi == n_gy - 1
        own_flat = xi * n_gy * n_gz + yi * n_gz + self.gz
        self.first_owner = own_flat - (1 - even) * n_gy * n_gz
        self.second_owner = self.first_owner + n_gy * n_gz
        self.lane = lanes_of((24, 128))
        self.row = rows_of((24, 128))
        self.keep_row = jnp.where((self.row >= 20) & self.no_low_y, 0.0, 1.0)
        self.own_off = jnp.where(self.gz == 0, 8, 4)
        self.own_j = jnp.where(self.gz == 0, 0, 4)
        self.got_j = jnp.where(self.gz == 0, 8, 0)

    def y_part(self, v):
        high = jnp.where(self.no_high_y, 0.0, 1.0)
        low = jnp.where(self.no_low_y, 0.0, 1.0)
        return v * jnp.where(rows_of(v.shape[-2:]) < EDGE, high, low)

    def strip_own(self, planes):
        lane = self.lane
        acc = jnp.zeros((24, 128), F32)
        for x, plane in enumerate(planes):
            acc = jnp.where(lane // 16 == x, pltpu.roll(plane, (16 * x + self.own_off) % 128, 1), acc)
        j = lane % 16
        return jnp.where((j >= self.own_j) & (j < self.own_j + 8), acc, 0.0)

    def strip_got(self, tile, got, q):
        j = self.lane % 16
        got = pltpu.roll(got, (self.got_j - 4 * (q % 4) + 128) % 128, 1)
        return jnp.where((j >= self.got_j) & (j < self.got_j + EDGE), got, tile)

    def with_seam(self, plane, strip, x):
        lane = lanes_of((16, 128))
        lo = jnp.where(self.gz == 0, 128 - EDGE, 0)
        moved = pltpu.roll(strip, (lo - 16 * x - EDGE + 256) % 128, 1)
        return jnp.where((lane >= lo) & (lane < lo + EDGE), moved, plane)

    def z_up(self, v):
        return jnp.where(self.lane == 127, 0.0, roll_up(v, 1))

    def z_down(self, v):
        return jnp.where(self.lane == 0, 0.0, roll_down(v, 1))


def y_up(v):
    return roll_up(v, 0)


def y_down(v):
    return roll_down(v, 0)


def sz_up(v):
    return roll_up(v, 1)


def sz_down(v):
    return roll_down(v, 1)


def parts_of(xs):
    return [xs[i : i + GROUP] for i in range(0, len(xs), GROUP)]


def get(ref, x, comps=(0, 1, 2)):
    return tuple(ref[c, x] for c in comps)


def put(ref, xs, values):
    for x, v in zip(xs, values):
        for c in range(3):
            ref[c, x] = v[c]


def sget(ref):
    return tuple(ref[c] for c in range(3))


def sput(ref, v):
    for c in range(3):
        ref[c] = v[c]


def pack_kernel(ip_hbm, sd_hbm, e_hbm, h_hbm, a_out, b_out, z_out, y_out, ip, sd, e, h, sems):
    even, gz = (lax.axis_index("gx") + 1) % 2, lax.axis_index("gz")
    refs = (ip, sd, e, h)
    copies = []
    for i, src in enumerate((ip_hbm, sd_hbm, e_hbm, h_hbm)):
        copies.append(pltpu.make_async_copy(src, refs[i], sems.at[i]))
    for copy in copies:
        copy.start()
    for copy in copies:
        copy.wait()
    cx = e.shape[1]
    a_base = jnp.where(even == 1, cx - DEEP, 0)
    b_base = jnp.where(even == 1, 0, cx - DEEP)
    for f in (PERM, SEED):
        for c in range(3):
            off = DEEP * (3 * f + c)
            a_out[off : off + DEEP] = refs[f][c, pl.ds(a_base, DEEP)]
            b_out[off : off + DEEP] = refs[f][c, pl.ds(b_base, DEEP)]
    group = lanes_of((16, 128)) // EDGE
    z_off = jnp.where(gz == 0, EDGE, 0)
    for t in range(3):
        total = jnp.zeros((16, 128), F32)
        for k in range(4):
            f, c = divmod(4 * t + k, 3)
            for x in range(cx):
                moved = pltpu.roll(refs[f][c, x], (16 * x + 4 * k + z_off) % 128, 1)
                total = jnp.where(group == 4 * x + k, moved, total)
        z_out[t] = total
    first = rows_of((cx, 8, 128)) < EDGE
    for f in range(4):
        for c in range(3):
            q = 3 * f + c
            y_out[q * cx : (q + 1) * cx] = jnp.where(first, refs[f][c, :, 0:8], refs[f][c, :, 8:16])


def own_kernel(ip_in, e_in, h_in, y1, z_in, yz,
               a_out, b_out, c_out, e_out, sc_out, se_out, si_out, I, E, H):
    at = Place()
    cx = e_in.shape[1]
    lane = at.lane
    zero = jnp.zeros((24, 128), F32)
    strips = []
    for f, X, src in ((PERM, I, ip_in), (ELEC, E, e_in), (MAGN, H, h_in)):
        strip = []
        for c in range(3):
            q = 3 * f + c
            X[c, 0] = zero
            X[c, cx + 1] = zero
            X[c, 1 : cx + 1, 0:16] = src[c]
            X[c, 1 : cx + 1, 16:24] = at.y_part(y1[q * cx : (q + 1) * cx])
            if f == PERM:
                X[c] = time_step * X[c]
            got = jnp.concatenate([z_in[q // 4], at.y_part(yz[q // 4])], axis=0)
            tile = at.strip_own([X[c, x] for x in range(1, cx + 1)])
            tile = at.strip_got(tile, time_step * got if f == PERM else got, q)
            strip.append(tile)
        strips.append(tuple(strip))
    si, se, sh = strips

    def sx_up(v):
        return jnp.where(lane >= 112, 0.0, pltpu.roll(v, 112, 1))

    def sx_down(v):
        return jnp.where(lane < 16, 0.0, pltpu.roll(v, 16, 1))

    xs = list(range(1, cx + 1))
    up_strip, down_strip = zero, zero
    for n in range(STEPS):
        downs = get(E, 1, (1, 2))
        keep = time_step * at.keep_row
        for part in parts_of(xs):
            new = []
            for x in part:
                curl = curl_f(get(E, x), get(E, x + 1, (1, 2)), y_up, at.z_up)
                new.append(tuple(q - keep * v for q, v in zip(get(H, x), curl)))
            put(H, part, new)
        curl = curl_f(se, (sx_up(se[1]), sx_up(se[2])), y_up, sz_up)
        down_from = se
        sh = tuple(q - time_step * at.keep_row * v for q, v in zip(sh, curl))
        ups = get(H, cx, (1, 2))
        for part in parts_of(xs):
            new, curls = [], []
            for x in part:
                curl = curl_b(get(H, x), get(H, x - 1, (1, 2)), y_down, at.z_down)
                new.append(tuple(q + i * v for q, i, v in zip(get(E, x), get(I, x), curl)))
                curls.append(curl)
            put(E, part, new)
            for x, curl in zip(part, curls):
                for c in range(3):
                    c_out[n, c, x - 1] = curl[c][0:16]
        curl = curl_b(sh, (sx_down(sh[1]), sx_down(sh[2])), y_down, sz_down)
        se = tuple(q + i * v for q, i, v in zip(se, si, curl))
        for c in range(3):
            sc_out[n, c] = curl[c]
        for k in range(2):
            i = 2 * n + k
            a_out[i] = jnp.where(at.even, ups[k], downs[k])
            b_out[i] = jnp.where(at.even, downs[k], ups[k])
            here = lane // 16 == i
            up_strip = jnp.where(here, pltpu.roll(sh[1 + k], (16 * i + 16) % 128, 1), up_strip)
            down_strip = jnp.where(here, pltpu.roll(down_from[1 + k], 16 * i, 1), down_strip)
    edges = [jnp.concatenate([z_in[t], at.y_part(yz[t])], axis=0) for t in range(2)]
    up_edges = jnp.where(lane < 64, pltpu.roll(edges[0], 64, 1), edges[1])
    down_edges = jnp.where(lane < 64, edges[0], pltpu.roll(edges[1], 64, 1))
    a_out[N_TRACES + 1] = jnp.where(at.even, up_edges, down_edges)
    b_out[N_TRACES + 1] = jnp.where(at.even, down_edges, up_edges)
    a_out[N_TRACES] = jnp.where(at.even, up_strip, down_strip)
    b_out[N_TRACES] = jnp.where(at.even, down_strip, up_strip)
    for c in range(3):
        e_out[c] = E[c, 1 : cx + 1, 0:16]
    sput(se_out, se)
    sput(si_out, si)


def adjoint_kernel(ip_in, sd_in, a_in, b_in, z_in, y1, yz, y2,
                   s_out, I, W, M, PS):
    at = Place()
    cx = ip_in.shape[1]
    lane = at.lane
    last = cx + 2 * DEEP
    top = STEPS - 1
    a_base = jnp.where(at.even, DEEP + cx, 0)
    b_base = jnp.where(at.even, 0, DEEP + cx)
    for f, X, src in ((PERM, I, ip_in), (SEED, PS.at[top], sd_in)):
        for c in range(3):
            q = 3 * f + c
            off = DEEP * q
            X[c, last] = jnp.zeros((24, 128), F32)
            X[c, DEEP : DEEP + cx, 0:16] = src[c]
            X[c, DEEP : DEEP + cx, 16:24] = at.y_part(y1[q * cx : (q + 1) * cx])
            X[c, pl.ds(a_base, DEEP), 0:16] = a_in[off : off + DEEP]
            X[c, pl.ds(a_base, DEEP), 16:24] = at.y_part(y2[off : off + DEEP])
            X[c, pl.ds(b_base, DEEP), 0:16] = b_in[off : off + DEEP]
            X[c, pl.ds(b_base, DEEP), 16:24] = at.y_part(y2[N_SLOTS + off : N_SLOTS + off + DEEP])
    for f, X in ((PERM, I), (SEED, PS.at[top])):
        for c in range(3):
            q = 3 * f + c
            t = q // 4
            own = jnp.concatenate([z_in[t], at.y_part(yz[t])], axis=0)
            around = [X[c, DEEP + cx + k] for k in range(DEEP)] + [jnp.zeros((24, 128), F32)] * 2
            around += [X[c, k] for k in range(DEEP)]
            if f == SEED:
                s_out[q, :, 0:128] = at.strip_got(at.strip_own([X[c, DEEP + x] for x in range(cx)]), own, q)
            s_out[q, :, 128:256] = at.strip_own(around)

    def keep_at(x):
        return at.keep_row * jnp.where(at.no_low_x, 0.0, 1.0) if x < DEEP else at.keep_row

    def sweep(lo, hi, body):
        for first in range(lo, hi, GROUP):
            body(list(range(first, min(first + GROUP, hi))))

    def halve(xs):
        new = []
        for x in xs:
            half = tuple(time_step * v for v in get(I, x))
            new.append((half, tuple(a * b for a, b in zip(half, get(PS.at[top], x)))))
        put(I, xs, [n[0] for n in new])
        put(W, xs, [n[1] for n in new])

    sweep(0, last, halve)
    for c in range(3):
        W[c, last] = jnp.zeros((24, 128), F32)

    for m in range(STEPS - 1):
        n = top - m

        def magnetic(xs, m=m):
            new = []
            for x in xs:
                curl = curl_f(get(W, x), get(W, x + 1, (1, 2)), y_up, at.z_up)
                keep = keep_at(x)
                if m == 0:
                    new.append(tuple(keep * v for v in curl))
                else:
                    new.append(tuple(q + keep * v for q, v in zip(get(M, x), curl)))
            put(M, xs, new)

        def electric(xs, m=m, n=n):
            new = []
            for x in xs:
                curl = curl_b(get(M, x), get(M, x - 1, (1, 2)), y_down, at.z_down)
                p = tuple(q - time_step * v for q, v in zip(get(PS.at[n], x), curl))
                new.append((p, tuple(a * b for a, b in zip(get(I, x), p))))
            put(PS.at[n - 1], xs, [v[0] for v in new])
            if m < STEPS - 2:
                put(W, xs, [v[1] for v in new])

        yield
        sweep(m, last - 1 - m, magnetic)
        yield
        sweep(m + 1, last - 1 - m, electric)


LOW_H = ([-1], [-2, -1, 0], [-2, -1, 0, 1], [-1, 0, 1, 2])
LOW_E = ([-1, 0], [-2, -1, 0, 1], [-1, 0, 1, 2], [0, 1, 2, 3])
HIGH_H = ([-1], [-2, -1, 0], [-3, -2, -1, 0], [-4, -3, -2, -1])
HIGH_E = ([-1, 0], [-2, -1, 0, 1], [-3, -2, -1, 0], [-4, -3, -2, -1])


def driven_kernel(a_sent, b_sent, high_in, low_in, e_own, sc_own, se_own, si_own, s_in, I, e_out, se_out, sg_out, E, H, CD):
    at = Place()
    cx = e_own.shape[1]
    lane = at.lane
    base = 3
    zero = jnp.zeros((24, 128), F32)
    for c in range(3):
        for x in range(E.shape[1]):
            E[c, x] = zero
            H[c, x] = zero

    def traces(a, b, i):
        return jnp.where(at.even, a[i], b[i])

    def upper(i):
        return high_in[i]

    def lower(i):
        return low_in[i]

    def own_up(i):
        return traces(a_sent, b_sent, i)

    def own_down(i):
        return traces(b_sent, a_sent, i)

    s_upper, s_lower, s_own_up, s_own_down = (t(N_TRACES) for t in (upper, lower, own_up, own_down))
    s_shape = (24, 256)
    s_keep = jnp.where((rows_of(s_shape) >= 20) & at.no_low_y, 0.0, time_step)
    s_keep = jnp.where((lanes_of(s_shape) >= 192) & at.no_low_x, 0.0, s_keep)

    def source(first, second, i, group):
        tiles = [pltpu.roll(v, (16 * (group - i)) % 128, 1) for v in (first, second)]
        return jnp.concatenate([jnp.where(lane // 16 == group, v, 0.0) for v in tiles], axis=1)

    above, below = upper(N_TRACES + 1), lower(N_TRACES + 1)
    edges = (
        jnp.where(lane < 64, above, pltpu.roll(below, 64, 1)),
        jnp.where(lane < 64, pltpu.roll(above, 64, 1), below),
    )
    strips = []
    for q in range(6):
        tile = at.strip_got(s_in[q, :, 128:256], edges[q // 4], q)
        first = si_own[q] if q < 3 else s_in[q, :, 0:128]
        strips.append(jnp.concatenate([first, time_step * tile if q < 3 else tile], axis=1))
    si = tuple(strips[0:3])
    sp = tuple(strips[3:6])
    adjoint = [None] * (STEPS - 1) + [sp]
    sm = (0.0, 0.0, 0.0)
    s_curls = []
    se = sh = (jnp.zeros(s_shape, F32),) * 3
    for n in range(STEPS):
        yield
        xs = LOW_H[n] + [cx + x for x in HIGH_H[n]]
        for part in parts_of(xs):
            new = []
            for x in part:
                nxt = get(E, base + x + 1, (1, 2))
                if x == -1:
                    nxt = tuple(v + own_down(2 * n + k) for k, v in enumerate(nxt))
                if x == cx - 1:
                    nxt = tuple(v + upper(2 * n + k) for k, v in enumerate(nxt))
                curl = curl_f(get(E, base + x), nxt, y_up, at.z_up)
                keep = time_step * at.keep_row
                if x < 0:
                    keep = keep * jnp.where(at.no_low_x, 0.0, 1.0)
                new.append(tuple(q - keep * v for q, v in zip(get(H, base + x), curl)))
            put(H, [base + x for x in part], new)
        nxt = tuple(pltpu.roll(se[1 + k], 240, 1) + source(s_upper, s_own_down, 2 * n + k, 7) for k in range(2))
        curl = curl_f(se, nxt, y_up, sz_up)
        sh = tuple(q - s_keep * v for q, v in zip(sh, curl))
        if n < STEPS - 1:
            sw = tuple(a * b for a, b in zip(si, sp))
            curl = curl_f(sw, [pltpu.roll(v, 240, 1) for v in sw[1:]], y_up, sz_up)
            sm = tuple(q + 2.0 * s_keep * v for q, v in zip(sm, curl))

        yield
        xs = LOW_E[n] + [cx + x for x in HIGH_E[n]]
        for part in parts_of(xs):
            new, grads = [], []
            for x in part:
                prv = get(H, base + x - 1, (1, 2))
                if x == 0:
                    prv = tuple(v + lower(2 * n + k) for k, v in enumerate(prv))
                if x == cx:
                    prv = tuple(v + own_up(2 * n + k) for k, v in enumerate(prv))
                curl = curl_b(get(H, base + x), prv, y_down, at.z_down)
                new.append(tuple(q + i * v for q, i, v in zip(get(E, base + x), get(I, DEEP + x), curl)))
                grads.append(curl)
            put(E, [base + x for x in part], new)
            for x, curl in zip(part, grads):
                if 0 <= x < cx:
                    for c in range(3):
                        CD[n, c, x] = curl[c][0:16]
        prv = tuple(pltpu.roll(sh[1 + k], 16, 1) + source(s_lower, s_own_up, 2 * n + k, 0) for k in range(2))
        curl = curl_b(sh, prv, y_down, sz_down)
        se = tuple(q + i * v for q, i, v in zip(se, si, curl))
        s_curls.append(tuple(v[:, 0:128] for v in curl))
        if n < STEPS - 1:
            curl = curl_b(sm, [pltpu.roll(v, 16, 1) for v in sm[1:]], y_down, sz_down)
            sp = tuple(q - time_step * v for q, v in zip(sp, curl))
            adjoint[STEPS - 2 - n] = sp
    for c in range(3):
        se_out[c] = se[c][0:16, 0:128] + se_own[c, 0:16]
        e_out[c] = E[c, base : base + cx, 0:16] + e_own[c]
        sg_out[c] = sum(adjoint[n][c][0:16, 0:128] * (s_curls[n][c] + sc_own[n, c])[0:16] for n in range(STEPS))
    yield


def sums_kernel(PS, c_own, CD, sg, ids, s_out):
    at = Place()
    cx = ids.shape[0]
    acc = jnp.zeros((80, 128), F32)
    for x in range(cx):
        grads = []
        for c in range(3):
            g = 0.0
            for n in range(STEPS):
                curl = c_own[n, c, x]
                if x in LOW_E[n] or x - cx in HIGH_E[n]:
                    curl = curl + CD[n, c, x]
                g = g + PS[n, c, DEEP + x, 0:16] * curl
            grads.append(at.with_seam(g, sg[c], x))
        lhs, rhs = [], []
        for r in range(2):
            g = jnp.concatenate([v[8 * r : 8 * r + 8] for v in grads], axis=0)
            one = g.astype(jnp.bfloat16).astype(F32)
            rest = g - one
            two = rest.astype(jnp.bfloat16).astype(F32)
            three = rest - two
            lhs.append(jnp.concatenate([one, two, three, jnp.zeros((8, 128), F32)], axis=0).astype(jnp.bfloat16))
            region = ids[x, 8 * r : 8 * r + 8]
            slot = jnp.where(
                region < at.second_owner * REG_DEV,
                region - at.first_owner * REG_DEV,
                region - at.second_owner * REG_DEV + REG_DEV,
            )
            hot = jnp.concatenate([jnp.where(slot == s, 1.0, 0.0) for s in range(2 * REG_DEV)], axis=0)
            rhs.append(hot.astype(jnp.bfloat16))
        acc = acc + lax.dot_general(
            jnp.concatenate(lhs, axis=1),
            jnp.concatenate(rhs, axis=1),
            (((1,), (1,)), ((), ())),
            preferred_element_type=F32,
        )
    sums = acc[0:24] + acc[24:48] + acc[48:72]
    sums = jnp.where(rows_of((24, 128)) % 8 == lanes_of((24, 128)) % 8, sums, 0.0)
    parts = [jnp.sum(sums[8 * c : 8 * c + 8], axis=0, keepdims=True) for c in range(3)]
    parts = jnp.concatenate(parts + [jnp.zeros((5, 128), F32)], axis=0)
    one = parts.astype(jnp.bfloat16).astype(F32)
    two = (parts - one).astype(jnp.bfloat16).astype(F32)
    split = jnp.concatenate([one, two, (parts - one) - two, jnp.zeros((8, 128), F32)], axis=0).astype(jnp.bfloat16)
    fold = jnp.where(rows_of((128, 128)) // 8 == lanes_of((128, 128)), 1.0, 0.0).astype(jnp.bfloat16)
    folded = jnp.dot(split, fold, preferred_element_type=F32)
    s_out[...] = (folded[0:8] + folded[8:16] + folded[16:24]) * (time_step * grad_scale)


def last_kernel(ip_in, sd_in, a_got, b_got, z_in, y1, yz, y2, c_own, a_sent, b_sent, high_in, low_in, e_own, sc_own, se_own, si_own, ids,
                e_out, se_out, s_out, I, W, M, PS, E, H, CD, s_ext, sg):
    runs = (
        adjoint_kernel(ip_in, sd_in, a_got, b_got, z_in, y1, yz, y2, s_ext, I, W, M, PS),
        driven_kernel(a_sent, b_sent, high_in, low_in, e_own, sc_own, se_own, si_own, s_ext, I, e_out, se_out, sg, E, H, CD),
    )
    for _ in range(2 * STEPS + 1):
        for run in runs:
            next(run, None)
    sums_kernel(PS, c_own, CD, sg, ids, s_out)


def finish_kernel(e_in, se_in, e_out):
    at = Place()
    for c in range(3):
        for x in range(e_in.shape[1]):
            e_out[c, x] = at.with_seam(e_in[c, x], se_in[c], x)


def y_rows(v):
    first = lax.broadcasted_iota(jnp.int32, (1, 8, 1), 1) < EDGE
    return jnp.where(first, v[:, 0:8], v[:, 8:16])


def local(e_start, h_start, inv_perm, adj_seed, region_ids):
    n_gx, n_gy = lax.axis_size("gx"), lax.axis_size("gy")
    xi = lax.axis_index("gx")
    cx = e_start.shape[1]
    even = (xi + 1) % 2
    vmem = pl.BlockSpec(memory_space=pltpu.VMEM)
    shape = lambda *dims: jax.ShapeDtypeStruct(dims, F32)
    tile = lambda *dims: pltpu.VMEM(dims, F32)

    a_pairs = [(i, i ^ 1) for i in range(n_gx)]
    b_pairs = [(i, ((i - 1) ^ 1) + 1) for i in range(1, n_gx - 1)]

    def swap_y(v):
        if n_gy == 2:
            return lax.ppermute(v, "gy", [(0, 1), (1, 0)])
        up = lax.ppermute(v, "gy", [(i, i + 1) for i in range(n_gy - 1)])
        down = lax.ppermute(v, "gy", [(i + 1, i) for i in range(n_gy - 1)])
        first = lax.broadcasted_iota(jnp.int32, (1, 8, 1), 1) < EDGE
        return jnp.where(first, down, up)

    def call(kernel, outs, scratch, args, mib, specs=None, cost=None):
        return pl.pallas_call(
            kernel,
            out_shape=outs,
            in_specs=specs or [vmem] * len(args),
            out_specs=(vmem,) * len(outs),
            scratch_shapes=scratch,
            cost_estimate=cost,
            compiler_params=pltpu.CompilerParams(vmem_limit_bytes=mib * 1024 * 1024),
        )(*args)

    own = tile(*e_start.shape)
    a_msg, b_msg, z_msg, y_msg = call(
        pack_kernel,
        (shape(N_SLOTS, 16, 128), shape(N_SLOTS, 16, 128), shape(3, 16, 128), shape(12 * cx, 8, 128)),
        [own] * 4 + [pltpu.SemaphoreType.DMA((4,))],
        tuple(pltpu.with_memory_space_constraint(v, pltpu.HBM) for v in (inv_perm, adj_seed, e_start, h_start)),
        8,
        [pl.BlockSpec(memory_space=pltpu.HBM)] * 4,
    )
    z_got = lax.ppermute(z_msg, "gz", [(0, 1), (1, 0)])
    y1 = swap_y(y_msg)
    a_got = lax.ppermute(a_msg, "gx", a_pairs)
    b_got = lax.ppermute(b_msg, "gx", b_pairs)
    yz = swap_y(y_rows(z_got))

    n_msg = N_TRACES + 2
    field = tile(3, cx + 2, 24, 128)
    a_sent, b_sent, c_own, e_own, sc_own, se_own, si_own = call(
        own_kernel,
        (
            shape(n_msg, 24, 128),
            shape(n_msg, 24, 128),
            shape(STEPS, 3, cx, 16, 128),
            shape(3, cx, 16, 128),
            shape(STEPS, 3, 24, 128),
            shape(3, 24, 128),
            shape(3, 24, 128),
        ),
        [field] * 3,
        (inv_perm, e_start, h_start, y1, z_got, yz),
        8,
    )
    a_in = lax.ppermute(a_sent, "gx", a_pairs)
    b_in = lax.ppermute(b_sent, "gx", b_pairs)
    high_in = jnp.where(even == 1, a_in, b_in)
    low_in = jnp.where(even == 1, b_in, a_in)
    y2 = swap_y(jnp.concatenate([y_rows(v) for v in (a_got, b_got)], axis=0))

    planes = cx + 2 * DEEP + 1
    field = tile(3, planes, 24, 128)
    driven = tile(3, cx + 5, 24, 128)
    e_main, e_strip, sums = call(
        last_kernel,
        (shape(*e_start.shape), shape(3, 16, 128), shape(8, 128)),
        [field] * 3
        + [tile(STEPS, 3, planes, 24, 128)]
        + [driven] * 2
        + [tile(STEPS, 3, cx, 16, 128), tile(6, 24, 256), tile(3, 16, 128)],
        (inv_perm, adj_seed, a_got, b_got, z_got, y1, yz, y2, c_own, a_sent, b_sent, high_in, low_in, e_own, sc_own, se_own, si_own, region_ids),
        16,
    )
    (e_field,) = call(finish_kernel, (shape(*e_start.shape),), [], (e_main, e_strip), 4)
    total = sums + lax.ppermute(sums, "gx", a_pairs)
    owned = jnp.where(even == 1, total[0:3, 0:REG_DEV], total[0:3, REG_DEV : 2 * REG_DEV])
    return e_field, owned


def solution(mesh):
    placed = (
        P(None, "gx", "gy", "gz"),
        P(None, "gx", "gy", "gz"),
        P(None, "gx", "gy", "gz"),
        P(None, "gx", "gy", "gz"),
        P("gx", "gy", "gz"),
    )
    return jax.shard_map(
        local,
        mesh=mesh,
        in_specs=placed,
        out_specs=(P(None, "gx", "gy", "gz"), P(None, ("gx", "gy", "gz"))),
        check_vma=False,
    )
```
